512 devices in a mesh: dp: 2 (over y_hi), fsdp: 32 (over z, core), tensor: 8 (over y_lo, x).
Axes of the slice: x: 4, y: 4 (y_hi: 2, y_lo: 2; y = y_hi * 2 + y_lo), z: 16, core: 2. Of those that a mesh axis runs over, the one named last changes fastest.
Arguments:
- tokens: bfloat16 [1024, 8192], P(('dp', 'fsdp'), 'tensor'), may hold values from -6 to 6
- base_weight: bfloat16 [2, 8192, 24576], P(None, 'tensor', 'fsdp'), may hold values from -0.0625 to 0.0625
- factor_b: bfloat16 [2, 8192, 64], P(None, 'tensor'), may hold values from -0.0625 to 0.0625
- factor_a: bfloat16 [2, 64, 24576], P(None, None, 'fsdp'), may hold values from -0.75 to 0.75
- magnitude: float32 [2, 24576], P(None, 'fsdp'), may hold values from 0.5 to 2
- cotangent: bfloat16 [1024, 24576], P(('dp', 'tensor'), 'fsdp'), may hold values from -6 to 6
Outputs:
- grad_a: float32 [2, 64, 24576], P(None, None, 'fsdp')
- grad_b: float32 [2, 8192, 64], P(None, 'tensor')
- grad_m: float32 [2, 24576], P(None, 'fsdp')
The draws below stay inside these ranges and needn't reach their ends.
All inputs are finite; a program needn't handle non-finite values.
Results may differ from the reference program's by a relative error of at most 0.0003.
Values may be sent and summed in bfloat16 or wider, within the bound.
No kernel may reach another device: no remote copies, remote signals or barrier semaphores. Data moves between devices by JAX's collectives and lax.ppermute only.
A program may use at most 64 MiB of HBM per device.

```python
import math
import jax
import jax.numpy as jnp
from jax import lax

D = 8192
FF = 24576
R = 64
TOKENS = 1024


def block_levels(stream_key, shape, pieces, smallest, largest):
    def one(dim, shards_of):
        heights = jax.random.uniform(jax.random.fold_in(jax.random.fold_in(stream_key, 6), dim), (shards_of,), jnp.float32, smallest / len(pieces), largest / len(pieces))
        return jnp.repeat(jnp.exp(heights), shape[dim] // shards_of).reshape((-1,) + (1,) * (len(shape) - dim - 1))

    gain = one(*pieces[0])
    for cut in pieces[1:]:
        gain = gain * one(*cut)
    return gain


def bell_draw(key, extent, scale, limit, pieces=(), dtype=jnp.bfloat16):
    result = jax.random.normal(key, extent, jnp.float32) * scale
    if len(pieces) > 0:
        result = block_levels(key, extent, pieces, -0.22, 0.18) * result
    return jnp.clip(result, min=-limit, max=limit).astype(dtype)


def setup_inputs(seed: int = 0) -> dict:
    key_list = jax.random.split(jax.random.key(seed), 7)
    tokens = bell_draw(key_list[0], (TOKENS, D), 1.0, 6.0, ((0, 64), (1, 8)))
    base_weight = bell_draw(key_list[1], (2, D, FF), D ** -0.5, 0.0625, ((1, 8), (2, 32)))
    factor_b = bell_draw(key_list[2], (2, D, R), D ** -0.5, 0.0625, ((1, 8),))
    factor_a = bell_draw(key_list[3], (2, R, FF), R ** -0.5, 0.75, ((2, 32),))
    magnitude = jnp.clip(jnp.exp(math.log(2.0) - 1.3862944 * jax.random.uniform(key_list[4], (2, FF), jnp.float32) ** block_levels(key_list[4], (2, FF), ((1, 32),), -0.2, 0.2)), 0.5, 2.0)
    cotangent = bell_draw(key_list[5], (TOKENS, FF), 1.0, 6.0, ((0, 16), (1, 32)))
    return {"tokens": tokens, "base_weight": base_weight, "factor_b": factor_b, "factor_a": factor_a, "magnitude": magnitude, "cotangent": cotangent}


def reference(tokens, base_weight, factor_b, factor_a, magnitude, cotangent):
    highest = lax.Precision.HIGHEST
    states = []
    for k in range(2):
        combined = base_weight[k].astype(jnp.float32) + jnp.dot(factor_b[k], factor_a[k], preferred_element_type=jnp.float32)
        norm = jnp.sqrt(lax.optimization_barrier(jnp.sum(combined * combined, axis=0)) + 1e-06)
        low = jnp.dot(tokens, factor_b[k], preferred_element_type=jnp.float32)
        pre = jnp.dot(tokens, base_weight[k], preferred_element_type=jnp.float32) + jnp.dot(low, factor_a[k].astype(jnp.float32), precision=highest)
        scale = magnitude[k] / norm
        states.append((combined, norm, low, pre, scale, pre * scale))
    gate = states[0][5]
    up_val = states[1][5]
    sig = jax.nn.sigmoid(gate)
    grad_h = cotangent.astype(jnp.float32)
    douts = [grad_h * up_val * sig * (1.0 + gate * (1.0 - sig)), grad_h * gate * sig]
    grads_a, grads_b, grads_m = ([], [], [])
    tokens_wide = tokens.astype(jnp.float32)
    for k in range(2):
        combined, norm, low, pre, scale, _ = states[k]
        dout = douts[k]
        grad_m = lax.optimization_barrier(jnp.sum(dout * pre, axis=0)) / norm
        coeff = -grad_m * magnitude[k] / (norm * norm)
        dpre = dout * scale
        a_wide = factor_a[k].astype(jnp.float32)
        grad_a = jnp.dot(low.T, dpre, precision=highest) + jnp.dot(factor_b[k].astype(jnp.float32).T, combined, precision=highest) * coeff
        back = jnp.dot(dpre, a_wide.T, precision=highest)
        grad_b = jnp.dot(tokens_wide.T, back, precision=highest) + jnp.dot(combined * coeff, a_wide.T, precision=highest)
        grads_a.append(grad_a)
        grads_b.append(grad_b)
        grads_m.append(grad_m)
    return (jnp.stack(grads_a), jnp.stack(grads_b), jnp.stack(grads_m))
```

```python
import jax
import jax.numpy as jnp
from jax import lax
from jax.sharding import Mesh, PartitionSpec as P

F32 = jnp.float32
BF16 = jnp.bfloat16
GROUP = ("dp", "tensor")


def split2(x):
    hi = x.astype(BF16)
    return hi, (x - hi.astype(F32)).astype(BF16)


def per_device(tokens, base, b, a, magnitude, cotangent):
    highest = lax.Precision.HIGHEST
    dp = lax.axis_index("dp")
    core = lax.axis_index("core")
    depth, columns = base.shape[1:]
    rank = a.shape[1]
    shards = lax.axis_size("tensor")
    zs = lax.axis_size("z")
    own = 2 * zs * tokens.shape[0] // shards
    half = own // 2
    swap = [(0, 1), (1, 0)]
    a_wide = a.astype(F32)

    g_own = lax.all_gather(tokens, "z", axis=0, tiled=True)
    g_other = lax.ppermute(g_own, "core", swap)

    combined = base.astype(F32) + jnp.einsum(
        "kdr,krf->kdf", b, a, preferred_element_type=F32
    )
    sq = jnp.sum(combined * combined, axis=1)
    cross = jnp.einsum("kdr,kdf->krf", b.astype(F32), combined, precision=highest)

    def forward(g):
        pre = jnp.einsum("td,kdf->tkf", g, base, preferred_element_type=F32)
        low = jnp.einsum("td,kdr->tkr", g, b, preferred_element_type=F32)
        return jnp.concatenate(
            [pre.reshape(-1, 2 * columns), low.reshape(-1, 2 * rank)], axis=1
        ).reshape(shards, half, 2 * (columns + rank))

    sq_row = jnp.pad(sq.reshape(1, 1, 2 * columns), ((0, 0), (0, 7), (0, 2 * rank)))
    payload = jnp.concatenate(
        [forward(g_own), forward(g_other), jnp.broadcast_to(sq_row, (shards,) + sq_row.shape[1:])],
        axis=1,
    )
    total = jnp.sum(lax.all_to_all(payload, "tensor", 0, 0), axis=0)
    base_own = total[:own, : 2 * columns].reshape(own, 2, columns)
    low = total[:own, 2 * columns :].reshape(own, 2, rank)
    norm = jnp.sqrt(total[own, : 2 * columns].reshape(2, columns) + 1e-06)

    pre = base_own + jnp.einsum("tkr,krf->tkf", low, a_wide, precision=highest)
    scale = magnitude / norm
    out = pre * scale[None]
    gate, up = out[:, 0], out[:, 1]
    sig = jax.nn.sigmoid(gate)
    cot = cotangent.reshape(2, 2, half // 2, columns)
    cot = jnp.where(core == 0, cot, cot[:, ::-1])
    grad_h = jnp.swapaxes(cot, 0, 1).reshape(own, columns).astype(F32)
    dout = jnp.stack(
        [grad_h * up * sig * (1.0 + gate * (1.0 - sig)), grad_h * gate * sig], axis=1
    )
    dpre = dout * scale[None]
    m_part = jnp.sum(dout * pre, axis=0)
    a_part = jnp.einsum("tkr,tkf->krf", low, dpre, precision=highest)
    back = jnp.einsum("tkf,krf->tkr", dpre, a_wide, precision=highest).reshape(own, 2 * rank)

    members = 2 * shards
    rows = 2 * rank // members
    tiles = columns // 128

    def tiled(x):
        return x.reshape(members, -1, tiles, 128).swapaxes(1, 2).reshape(members, -1, 128)

    def untiled(x):
        return x.reshape(x.shape[0], tiles, -1, 128).swapaxes(1, 2).reshape(x.shape[0], -1, columns)

    cross_half = lax.dynamic_index_in_dim(
        cross.reshape(members, 2, rows // 2, columns), dp, 1, keepdims=False
    )
    everyone = lambda x: jnp.broadcast_to(x[None], (members,) + x.shape)
    parts = [
        tiled(a_part),
        tiled(cross_half),
        everyone(jnp.pad(m_part.reshape(2 * tiles, 128), ((0, 4), (0, 0)))),
        everyone(back),
    ]
    cuts = [0]
    for part in parts:
        cuts.append(cuts[-1] + part.shape[1])
    got = lax.all_to_all(jnp.concatenate(parts, axis=1), GROUP, 0, 0)
    a_own = jnp.sum(untiled(got[:, cuts[0] : cuts[1]]), axis=0)
    cross_own = jnp.sum(
        untiled(got[:, cuts[1] : cuts[2]]).reshape(2, shards, rows // 2, columns), axis=1
    ).reshape(rows, columns)
    m_total = jnp.sum(got[:, cuts[2] : cuts[2] + 2 * tiles], axis=0).reshape(2, columns)
    backs = lax.dynamic_slice_in_dim(got[:, cuts[3] : cuts[4]], dp * shards, shards, 0)

    grad_m = m_total / norm
    coeff = -grad_m * magnitude / (norm * norm)

    my_k = lax.axis_index(GROUP) // (members // 2)
    a_rows = a_own + cross_own * lax.dynamic_index_in_dim(coeff, my_k, 0)
    grad_a = lax.all_to_all(everyone(a_rows), GROUP, 0, 0).reshape(2, rank, columns)

    token_b = lax.dot_general(
        backs[:, :half].reshape(-1, 2 * rank),
        g_own.astype(F32),
        (((0,), (0,)), ((), ())),
        precision=highest,
    ) + lax.dot_general(
        backs[:, half:].reshape(-1, 2 * rank),
        g_other.astype(F32),
        (((0,), (0,)), ((), ())),
        precision=highest,
    )
    token_b = token_b.reshape(2, rank, depth)
    weighted = lax.dynamic_index_in_dim(coeff[:, None] * a_wide, dp, 0, keepdims=False)
    value_b = lax.dot_general(
        weighted,
        lax.dynamic_index_in_dim(combined, dp, 0, keepdims=False),
        (((1,), (1,)), ((), ())),
        precision=highest,
    )
    mine = lax.dynamic_index_in_dim(token_b, core, 0, keepdims=False)
    theirs = lax.dynamic_index_in_dim(token_b, 1 - core, 0, keepdims=False)
    mine = jnp.where(core == dp, mine + value_b, mine)
    theirs = jnp.where(core == dp, theirs, theirs + value_b)
    part_b = mine + lax.ppermute(theirs, "core", swap)
    chunks = part_b.reshape(zs, -1, 128)
    piece = jnp.sum(lax.all_to_all(chunks, "z", 0, 0), axis=0)
    piece = piece + lax.ppermute(piece, "dp", swap)
    full = lax.all_to_all(jnp.broadcast_to(piece[None], chunks.shape), "z", 0, 0)
    full = full.reshape(rank, depth)
    other = lax.ppermute(full, "core", swap)
    grad_b = jnp.where(core == 0, jnp.stack([full, other]), jnp.stack([other, full]))
    return grad_a, jnp.swapaxes(grad_b, 1, 2), grad_m


def solution(mesh):
    sizes = mesh.shape
    fine = Mesh(
        mesh.devices.reshape(sizes["dp"], sizes["fsdp"] // 2, 2, sizes["tensor"]),
        ("dp", "z", "core", "tensor"),
    )
    fsdp = ("z", "core")
    return jax.shard_map(
        per_device,
        mesh=fine,
        in_specs=(
            P(("dp",) + fsdp, "tensor"),
            P(None, "tensor", fsdp),
            P(None, "tensor", None),
            P(None, None, fsdp),
            P(None, fsdp),
            P(GROUP, fsdp),
        ),
        out_specs=(P(None, None, fsdp), P(None, "tensor", None), P(None, fsdp)),
        check_vma=False,
    )
```

```python
import functools
import math

import jax
import jax.numpy as jnp
from jax import lax
from jax.experimental import pallas as pl
from jax.experimental.pallas import tpu as pltpu
from jax.sharding import Mesh, PartitionSpec as P

F32 = jnp.float32
BF16 = jnp.bfloat16
GROUP = ("dp", "tensor")
PARAMS = pltpu.CompilerParams(vmem_limit_bytes=48 * 2**20)
VMEM = pl.BlockSpec(memory_space=pltpu.VMEM)
SMEM = pl.BlockSpec(memory_space=pltpu.SMEM)

BEND = 4096.0
POWER = 250.0 / math.log2(1.0 + BEND)
SHIFT = 125.0 * math.log(2.0)


def encode(x, peak):
    size = jnp.exp(POWER * jnp.log(1.0 + jnp.abs(x) * (BEND / peak)) - SHIFT)
    return jnp.where(x < 0, -size, size).astype(BF16)


def decode(code, peak):
    code = code.astype(F32)
    size = (jnp.exp((jnp.log(jnp.abs(code)) + SHIFT) * (1.0 / POWER)) - 1.0) * (peak / BEND)
    return jnp.where(code < 0, -size, size)


def peak_of(x):
    peak = jnp.max(jnp.max(jnp.abs(x), axis=1, keepdims=True), axis=0, keepdims=True)
    return (jnp.maximum(peak, 1e-20) * 1.01).astype(BF16).astype(F32)


def split(x):
    hi = x.astype(BF16)
    return hi, (x - hi.astype(F32)).astype(BF16)


def dot(x, y, dims=((1,), (0,))):
    return lax.dot_general(x, y, (dims, ((), ())), preferred_element_type=F32)


NT = ((1,), (1,))
TN = ((0,), (0,))


def weights_kernel(base_ref, bt_ref, a_ref, cross_ref, extra_ref):
    depth, columns = base_ref.shape[1:]
    rank = a_ref.shape[1]
    tiles = columns // 128
    step = 256
    extra_ref[...] = jnp.zeros_like(extra_ref)
    for k in range(2):
        sq = jnp.zeros((1, columns), F32)
        cross = jnp.zeros((rank, columns), F32)
        for at in range(0, depth, step):
            rows = slice(at, at + step)
            bt = bt_ref[k, :, rows]
            combined = base_ref[k, rows, :].astype(F32) + dot(bt, a_ref[k], TN)
            sq += jnp.sum(combined * combined, axis=0, keepdims=True)
            hi, lo = split(combined)
            cross += dot(bt, hi) + dot(bt, lo)
        cross_ref[k * rank : (k + 1) * rank, :] = cross
        for piece in range(3):
            part = sq.astype(BF16).astype(F32)
            sq = sq - part
            for i in range(tiles):
                row = 2 * tiles * piece + tiles * k + i
                extra_ref[row : row + 1, :] = part[:, 128 * i : 128 * (i + 1)]


def forward_kernel(own_ref, other_ref, base_ref, bt_ref, extra_ref, out_ref):
    shards, owned, _ = out_ref.shape
    columns = base_ref.shape[2]
    half = owned // 2
    rank = bt_ref.shape[0]
    peaks = jnp.zeros((16, 128), F32)
    line = lax.broadcasted_iota(jnp.int32, (16, 128), 0)
    row = 0
    for side, ref in enumerate((own_ref, other_ref)):
        where = slice(side * half, (side + 1) * half)
        for k in range(3):
            if k < 2:
                value = dot(ref[...], base_ref[k])
                lanes = slice(k * columns, (k + 1) * columns)
            else:
                value = dot(ref[...], bt_ref[...], NT)
                lanes = slice(2 * columns, 2 * columns + rank)
            peak = peak_of(value)
            out_ref[:, where, lanes] = encode(value, peak).reshape(shards, half, value.shape[1])
            peaks = jnp.where(line == row, peak, peaks)
            row += 1
    tail = jnp.concatenate([extra_ref[...], peaks], axis=0).astype(BF16)
    out_ref[:, :, 2 * columns + rank :] = jnp.broadcast_to(tail[None], (shards,) + tail.shape)


def local_kernel(place_ref, got_ref, cot_ref, a_ref, mag_ref, cross_ref, out_ref, norm_ref):
    dp, core = place_ref[0], place_ref[1]
    shards, owned, _ = got_ref.shape
    rank, columns = a_ref.shape[1:]
    tiles = columns // 128
    half = owned // 2
    tail = 2 * columns + 2 * rank
    peak_rows = 3 * 2 * tiles + 12

    totals = []
    for k in range(3):
        lanes = slice(k * columns, (k + 1) * columns) if k < 2 else slice(2 * columns, tail)
        sides = []
        for side in range(2):
            total = None
            for source in range(shards):
                peaks = got_ref[source, peak_rows : peak_rows + 16, tail:].astype(F32)
                at = 3 * side + k
                value = decode(
                    got_ref[source, side * half : (side + 1) * half, lanes],
                    peaks[at : at + 1, 0:1],
                )
                total = value if total is None else total + value
            sides.append(total)
        totals.append(jnp.concatenate(sides, axis=0))
    extra = got_ref[0, :48, tail:].astype(F32)
    for source in range(1, shards):
        extra += got_ref[source, :48, tail:].astype(F32)
    pieces = extra[24:36] + extra[12:24] + extra[0:12]

    low = totals[2]
    low_hi, low_lo = split(low)
    outs, pres, scales = [], [], []
    for k in range(2):
        sq = jnp.concatenate(
            [pieces[tiles * k + i : tiles * k + i + 1] for i in range(tiles)], axis=1
        )
        norm = jnp.sqrt(sq + 1e-06)
        norm_ref[k : k + 1, :] = norm
        mine = slice(k * rank, (k + 1) * rank)
        pre = totals[k] + (dot(low_hi[:, mine], a_ref[k]) + dot(low_lo[:, mine], a_ref[k]))
        scale = mag_ref[k : k + 1, :] / norm
        pres.append(pre)
        scales.append(scale)
        outs.append(pre * scale)
    gate, up = outs
    quarter = half // 2
    cot = jnp.concatenate(
        [
            cot_ref[pl.ds(pl.multiple_of(start + side * quarter, quarter), quarter), :]
            for side in (core, 1 - core)
            for start in (0, half)
        ],
        axis=0,
    ).astype(F32)
    sig = 1.0 / (1.0 + jnp.exp(-gate))
    douts = (cot * up * sig * (1.0 + gate * (1.0 - sig)), cot * gate * sig)
    members = out_ref.shape[0]
    rows = 2 * rank // members
    at_cross = tiles * rows
    at_m = at_cross + tiles * rows // 2
    at_back = at_m + 16
    out_ref[:, at_m:at_back, :] = jnp.zeros((members, at_back - at_m, 128), F32)
    backs = []
    for k in range(2):
        mine = slice(k * rank, (k + 1) * rank)
        m = jnp.sum(douts[k] * pres[k], axis=0, keepdims=True)
        dpre = douts[k] * scales[k]
        hi, lo = split(dpre)
        grad_a = (
            dot(low_hi[:, mine], hi, TN) + dot(low_hi[:, mine], lo, TN) + dot(low_lo[:, mine], hi, TN)
        )
        backs.append(dot(hi, a_ref[k], NT) + dot(lo, a_ref[k], NT))
        for i in range(tiles):
            lanes = slice(128 * i, 128 * (i + 1))
            row = at_m + tiles * k + i
            out_ref[:, row : row + 1, :] = jnp.broadcast_to(m[None, :, lanes], (members, 1, 128))
            for j in range(members // 2):
                out_ref[k * members // 2 + j, rows * i : rows * (i + 1), :] = grad_a[
                    rows * j : rows * (j + 1), lanes
                ]
    for i in range(tiles // 2):
        lanes = pl.ds(pl.multiple_of((dp * (tiles // 2) + i) * 128, 128), 128)
        out_ref[:, at_cross + rows * i : at_cross + rows * (i + 1), :] = cross_ref[:, lanes].reshape(
            members, rows, 128
        )
    back = jnp.concatenate(backs, axis=1)
    out_ref[:, at_back:, :] = jnp.broadcast_to(back[None], (members,) + back.shape)


def coefficient_kernel(place_ref, got_ref, norm_ref, mag_ref, rows_ref, grad_m_ref, coeff_ref):
    members, rows, columns = rows_ref.shape
    tiles = columns // 128
    at_cross = tiles * rows
    at_m = at_cross + tiles * rows // 2
    m = jnp.sum(got_ref[:, at_m : at_m + 16, :], axis=0)
    for k in range(2):
        norm = norm_ref[k : k + 1, :]
        m_row = jnp.concatenate([m[tiles * k + i : tiles * k + i + 1] for i in range(tiles)], axis=1)
        grad_m = m_row / norm
        grad_m_ref[k : k + 1, :] = grad_m
        coeff_ref[k : k + 1, :] = -grad_m * mag_ref[k : k + 1, :] / (norm * norm)
    coeff = jnp.where(place_ref[0] == 0, coeff_ref[0:1, :], coeff_ref[1:2, :])
    for i in range(tiles):
        lanes = slice(128 * i, 128 * (i + 1))
        token = jnp.sum(got_ref[:, rows * i : rows * (i + 1), :], axis=0)
        source, tile = divmod(i, tiles // 2)
        at = at_cross + rows * tile
        sources = slice(source * members // 2, (source + 1) * members // 2)
        cross = jnp.sum(got_ref[sources, at : at + rows, :], axis=0)
        own = token + cross * coeff[:, lanes]
        rows_ref[:, :, lanes] = jnp.broadcast_to(own[None], (members, rows, 128))


def width_kernel(
    place_ref, got_ref, coeff_ref, own_ref, other_ref, base_ref, bt_ref, a_ref, mine_ref, theirs_ref, sum_ref
):
    dp, core = place_ref[0], place_ref[1]
    members = got_ref.shape[0]
    shards = members // 2
    rank = a_ref.shape[1]
    owned = 2 * own_ref.shape[0] // shards
    half = owned // 2
    at_back = got_ref.shape[1] - owned
    total = None
    for side, ref in enumerate((own_ref, other_ref)):
        rows = pl.ds(at_back + side * half, half)
        back = got_ref[pl.ds(dp * shards, shards), rows, :].reshape(shards * half, 2 * rank)
        hi, lo = split(back)
        both = dot(jnp.concatenate([hi, lo], axis=1), ref[...], TN)
        part = both[: 2 * rank] + both[2 * rank :]
        total = part if total is None else total + part
    sum_ref[...] = total
    a = a_ref[dp]
    hi, lo = split(a.astype(F32) * coeff_ref[pl.ds(dp, 1), :])
    weighted = jnp.concatenate([hi, lo], axis=0)
    both = dot(weighted, base_ref[dp], NT)
    small = dot(weighted, a, NT)
    small_hi, small_lo = split(small[:rank] + small[rank:])
    value = (both[:rank] + both[rank:]) + (dot(small_hi, bt_ref[dp]) + dot(small_lo, bt_ref[dp]))
    mine = pl.ds(pl.multiple_of(dp * rank, rank), rank)
    sum_ref[mine, :] += value
    width = mine_ref.shape[1]
    mine_ref[...] = sum_ref[:, pl.ds(pl.multiple_of(core * width, width), width)]
    theirs_ref[...] = sum_ref[:, pl.ds(pl.multiple_of((1 - core) * width, width), width)]


def call(kernel, outs, in_specs, flops=0, size=0, scratch=()):
    return pl.pallas_call(
        kernel,
        out_shape=outs,
        in_specs=in_specs,
        out_specs=[VMEM] * len(outs) if isinstance(outs, (list, tuple)) else VMEM,
        scratch_shapes=scratch,
        compiler_params=PARAMS,
        cost_estimate=pl.CostEstimate(flops=flops, bytes_accessed=size, transcendentals=0),
    )


def shape(dims, dtype=F32):
    return jax.ShapeDtypeStruct(dims, dtype)


def per_device(tokens, base, b, a, magnitude, cotangent):
    dp = lax.axis_index("dp")
    core = lax.axis_index("core")
    member = lax.axis_index(GROUP)
    depth, columns = base.shape[1:]
    rank = a.shape[1]
    shards = lax.axis_size("tensor")
    members = 2 * shards
    zs = lax.axis_size("z")
    own = 2 * zs * tokens.shape[0] // shards
    rows = 2 * rank // members
    tiles = columns // 128
    swap = [(0, 1), (1, 0)]
    bt = jnp.swapaxes(b, 1, 2)
    place = jnp.stack([dp, core]).astype(jnp.int32)
    my_k = jnp.reshape(member // shards, (1,)).astype(jnp.int32)

    g_own = lax.all_gather(tokens, "z", axis=0, tiled=True)
    g_other = lax.ppermute(g_own, "core", swap)
    cross, extra = call(
        weights_kernel,
        [shape((2 * rank, columns)), shape((48, 128))],
        [VMEM] * 3,
        flops=2 * 2 * depth * columns * rank * 3,
        size=4 * 2**20,
    )(base, bt, a)
    payload = call(
        forward_kernel,
        shape((shards, own, 2 * columns + 4 * rank), BF16),
        [VMEM] * 5,
        flops=2 * shards * own * depth * 2 * (columns + rank),
        size=8 * 2**20,
    )(g_own, g_other, base, bt.reshape(2 * rank, depth), extra)
    got = lax.all_to_all(payload, "tensor", 0, 0)

    height = tiles * rows + tiles * rows // 2 + 16 + own
    sends, norm = call(
        local_kernel,
        [shape((members, height, 128)), shape((2, columns))],
        [SMEM] + [VMEM] * 5,
        flops=2**27,
        size=4 * 2**20,
    )(place, got, cotangent, a, magnitude, cross)
    got = lax.all_to_all(sends, GROUP, 0, 0)

    a_rows, grad_m, coeff = call(
        coefficient_kernel,
        [shape((members, rows, columns)), shape((2, columns)), shape((2, columns))],
        [SMEM] + [VMEM] * 3,
        size=2 * 2**20,
    )(my_k, got, norm, magnitude)
    grad_a = lax.all_to_all(a_rows, GROUP, 0, 0).reshape(2, rank, columns)
    mine, theirs = call(
        width_kernel,
        [shape((2 * rank, depth // 2))] * 2,
        [SMEM] + [VMEM] * 7,
        flops=2**30,
        size=8 * 2**20,
        scratch=[pltpu.VMEM((2 * rank, depth), F32)],
    )(place, got, coeff, g_own, g_other, base, bt, a)

    part = mine + lax.ppermute(theirs, "core", swap)
    chunks = part.reshape(zs, 2 * rank // zs, depth // 2)
    piece = jnp.sum(lax.all_to_all(chunks, "z", 0, 0), axis=0)
    piece = piece + lax.ppermute(piece, "dp", swap)
    full = lax.all_to_all(jnp.broadcast_to(piece[None], chunks.shape), "z", 0, 0)
    full = full.reshape(2 * rank, depth // 2)
    other = lax.ppermute(full, "core", swap)
    grad_b = jnp.where(
        core == 0, jnp.concatenate([full, other], axis=1), jnp.concatenate([other, full], axis=1)
    )
    return grad_a, jnp.swapaxes(grad_b.reshape(2, rank, depth), 1, 2), grad_m


def solution(mesh):
    sizes = mesh.shape
    fine = Mesh(
        mesh.devices.reshape(sizes["dp"], sizes["fsdp"] // 2, 2, sizes["tensor"]),
        ("dp", "z", "core", "tensor"),
    )
    fsdp = ("z", "core")
    return jax.shard_map(
        per_device,
        mesh=fine,
        in_specs=(
            P(("dp",) + fsdp, "tensor"),
            P(None, "tensor", fsdp),
            P(None, "tensor", None),
            P(None, None, fsdp),
            P(None, fsdp),
            P(GROUP, fsdp),
        ),
        out_specs=(P(None, None, fsdp), P(None, "tensor", None), P(None, fsdp)),
        check_vma=False,
    )
```

```python
import math

import jax
import jax.numpy as jnp
from jax import lax
from jax.experimental import pallas as pl
from jax.experimental.pallas import tpu as pltpu
from jax.sharding import Mesh, PartitionSpec as P

F32 = jnp.float32
BF16 = jnp.bfloat16
GROUP = ("dp", "tensor")
PARAMS = pltpu.CompilerParams(vmem_limit_bytes=24 * 2**20)
VMEM = pl.BlockSpec(memory_space=pltpu.VMEM)
SMEM = pl.BlockSpec(memory_space=pltpu.SMEM)

BEND = 4096.0
POWER = 250.0 / math.log2(1.0 + BEND)
SHIFT = 125.0 * math.log(2.0)


def encode(x, peak):
    size = jnp.exp(POWER * jnp.log(1.0 + jnp.abs(x) * (BEND / peak)) - SHIFT)
    return jnp.where(x < 0, -size, size)


def decode(code, peak):
    code = code.astype(F32)
    size = (jnp.exp((jnp.log(jnp.abs(code)) + SHIFT) * (1.0 / POWER)) - 1.0) * (peak / BEND)
    return jnp.where(code < 0, -size, size)


def peak_of(x):
    peak = jnp.max(jnp.max(jnp.abs(x), axis=1, keepdims=True), axis=0, keepdims=True)
    return (jnp.maximum(peak, 1e-20) * 1.01).astype(BF16).astype(F32)


def split(x):
    hi = x.astype(BF16)
    return hi, (x - hi.astype(F32)).astype(BF16)


def dot(x, y, dims=((1,), (0,))):
    return lax.dot_general(x, y, (dims, ((), ())), preferred_element_type=F32)


NT = ((1,), (1,))
TN = ((0,), (0,))


def weights_kernel(base_ref, bt_ref, a_ref, cross_ref, extra_ref):
    depth, columns = base_ref.shape[1:]
    rank = a_ref.shape[1]
    tiles = columns // 128
    step = 256
    extra_ref[...] = jnp.zeros_like(extra_ref)
    for k in range(2):
        sq = jnp.zeros((1, columns), F32)
        cross = jnp.zeros((rank, columns), F32)
        for at in range(0, depth, step):
            rows = slice(at, at + step)
            bt = bt_ref[k, :, rows]
            combined = base_ref[k, rows, :].astype(F32) + dot(bt, a_ref[k], TN)
            sq += jnp.sum(combined * combined, axis=0, keepdims=True)
            hi, lo = split(combined)
            cross += dot(bt, hi) + dot(bt, lo)
        cross_ref[k * rank : (k + 1) * rank, :] = cross
        for piece in range(3):
            part = sq.astype(BF16).astype(F32)
            sq = sq - part
            for i in range(tiles):
                row = 2 * tiles * piece + tiles * k + i
                extra_ref[row : row + 1, :] = part[:, 128 * i : 128 * (i + 1)]


def forward_kernel(own_ref, other_ref, base_ref, bt_ref, extra_ref, out_ref):
    shards, owned, _ = out_ref.shape
    columns = base_ref.shape[2]
    half = owned // 2
    rank = bt_ref.shape[0]
    peaks = jnp.zeros((16, 128), F32)
    line = lax.broadcasted_iota(jnp.int32, (16, 128), 0)
    row = 0
    for side, ref in enumerate((own_ref, other_ref)):
        where = slice(side * half, (side + 1) * half)
        for k in range(3):
            if k < 2:
                value = dot(ref[...], base_ref[k])
                lanes = slice(k * columns, (k + 1) * columns)
            else:
                value = dot(ref[...], bt_ref[...], NT)
                lanes = slice(2 * columns, 2 * columns + rank)
            peak = peak_of(value)
            code = encode(value, peak).astype(BF16)
            out_ref[:, where, lanes] = code.reshape(shards, half, value.shape[1])
            peaks = jnp.where(line == row, peak, peaks)
            row += 1
    tail = jnp.concatenate([extra_ref[...], peaks], axis=0).astype(BF16)
    out_ref[:, :, 2 * columns + rank :] = jnp.broadcast_to(tail[None], (shards,) + tail.shape)


def local_kernel(place_ref, got_ref, cot_ref, a_ref, mag_ref, cross_ref, out_ref, norm_ref):
    dp, core = place_ref[0], place_ref[1]
    shards, owned, _ = got_ref.shape
    rank, columns = a_ref.shape[1:]
    tiles = columns // 128
    half = owned // 2
    tail = 2 * columns + 2 * rank
    peak_rows = 3 * 2 * tiles + 12

    totals = []
    for k in range(3):
        lanes = slice(k * columns, (k + 1) * columns) if k < 2 else slice(2 * columns, tail)
        sides = []
        for side in range(2):
            total = None
            for source in range(shards):
                peaks = got_ref[source, peak_rows : peak_rows + 16, tail:].astype(F32)
                at = 3 * side + k
                value = decode(
                    got_ref[source, side * half : (side + 1) * half, lanes],
                    peaks[at : at + 1, 0:1],
                )
                total = value if total is None else total + value
            sides.append(total)
        totals.append(jnp.concatenate(sides, axis=0))
    extra = got_ref[0, :48, tail:].astype(F32)
    for source in range(1, shards):
        extra += got_ref[source, :48, tail:].astype(F32)
    pieces = extra[24:36] + extra[12:24] + extra[0:12]

    low = totals[2]
    low_hi, low_lo = split(low)
    outs, pres, scales = [], [], []
    for k in range(2):
        sq = jnp.concatenate(
            [pieces[tiles * k + i : tiles * k + i + 1] for i in range(tiles)], axis=1
        )
        norm = jnp.sqrt(sq + 1e-06)
        norm_ref[k : k + 1, :] = norm
        mine = slice(k * rank, (k + 1) * rank)
        pre = totals[k] + (dot(low_hi[:, mine], a_ref[k]) + dot(low_lo[:, mine], a_ref[k]))
        scale = mag_ref[k : k + 1, :] / norm
        pres.append(pre)
        scales.append(scale)
        outs.append(pre * scale)
    gate, up = outs
    quarter = half // 2
    cot = jnp.concatenate(
        [
            cot_ref[pl.ds(pl.multiple_of(start + side * quarter, quarter), quarter), :]
            for side in (core, 1 - core)
            for start in (0, half)
        ],
        axis=0,
    ).astype(F32)
    sig = 1.0 / (1.0 + jnp.exp(-gate))
    douts = (cot * up * sig * (1.0 + gate * (1.0 - sig)), cot * gate * sig)
    members = out_ref.shape[0]
    rows = 2 * rank // members
    line = lax.broadcasted_iota(jnp.int32, (rows, 128), 0)
    codes, peaks, back_codes, back_peaks, ms = [], [], [], [], []
    for k in range(2):
        mine = slice(k * rank, (k + 1) * rank)
        ms.append(jnp.sum(douts[k] * pres[k], axis=0, keepdims=True))
        hi, lo = split(douts[k] * scales[k])
        grad_a = (
            dot(low_hi[:, mine], hi, TN) + dot(low_hi[:, mine], lo, TN) + dot(low_lo[:, mine], hi, TN)
        )
        back = dot(hi, a_ref[k], NT) + dot(lo, a_ref[k], NT)
        width = columns // 2
        cross = cross_ref[mine, pl.ds(pl.multiple_of(dp * width, width), width)]
        peaks.append((peak_of(grad_a), peak_of(cross)))
        codes.append((encode(grad_a, peaks[k][0]), encode(cross, peaks[k][1])))
        back_peaks.append(peak_of(back))
        back_codes.append(encode(back, back_peaks[k]))
    for j in range(members):
        k, at = divmod(j * rows, rank)
        blocks = [
            code[at : at + rows, 128 * i : 128 * (i + 1)]
            for code in codes[k]
            for i in range(code.shape[1] // 128)
        ]
        tail_block = jnp.zeros((rows, 128), F32)
        for row, peak in enumerate(peaks[k] + tuple(back_peaks)):
            tail_block = jnp.where(line == row, peak, tail_block)
        blocks.append(tail_block)
        for i in range(0, len(blocks), 2):
            pair = jnp.concatenate(blocks[i : i + 2], axis=0).astype(BF16)
            out_ref[j, rows * i : rows * (i + 2), :] = pair
    height = rows * (tiles + tiles // 2 + 1)
    lines = []
    for piece in range(2):
        for k in range(2):
            part = ms[k].astype(BF16).astype(F32)
            ms[k] = ms[k] - part
            lines += [part[:, 128 * i : 128 * (i + 1)] for i in range(tiles)]
    lines.append(jnp.zeros((32 - len(lines), 128), F32))
    rest = jnp.concatenate(lines + [jnp.concatenate(back_codes, axis=1)], axis=0).astype(BF16)
    out_ref[:, height:, :] = jnp.broadcast_to(rest[None], (members,) + rest.shape)


def coefficient_kernel(place_ref, got_ref, norm_ref, mag_ref, rows_ref, grad_m_ref, coeff_ref):
    members, rows, columns = rows_ref.shape
    tiles = columns // 128
    height = rows * (tiles + tiles // 2 + 1)
    m = jnp.sum(got_ref[:, height : height + 32, :].astype(F32), axis=0)
    m = m[: 2 * tiles] + m[2 * tiles : 4 * tiles]
    for k in range(2):
        norm = norm_ref[k : k + 1, :]
        m_row = jnp.concatenate([m[tiles * k + i : tiles * k + i + 1] for i in range(tiles)], axis=1)
        grad_m = m_row / norm
        grad_m_ref[k : k + 1, :] = grad_m
        coeff_ref[k : k + 1, :] = -grad_m * mag_ref[k : k + 1, :] / (norm * norm)
    coeff = jnp.where(place_ref[0] == 0, coeff_ref[0:1, :], coeff_ref[1:2, :])
    tokens = [jnp.zeros((rows, 128), F32)] * tiles
    crosses = [jnp.zeros((rows, 128), F32)] * tiles
    for j in range(members):
        blocks = got_ref[j, :height, :].astype(F32)
        peaks = blocks[height - rows :]
        token = decode(blocks[: rows * tiles], peaks[0:1, 0:1])
        cross = decode(blocks[rows * tiles : height - rows], peaks[1:2, 0:1])
        for i in range(tiles):
            tokens[i] = tokens[i] + token[rows * i : rows * (i + 1)]
        first = j * 2 // members * (tiles // 2)
        for i in range(tiles // 2):
            crosses[first + i] = crosses[first + i] + cross[rows * i : rows * (i + 1)]
    for i in range(tiles):
        lanes = slice(128 * i, 128 * (i + 1))
        own = tokens[i] + crosses[i] * coeff[:, lanes]
        rows_ref[:, :, lanes] = jnp.broadcast_to(own[None], (members, rows, 128))


def width_kernel(
    place_ref, got_ref, coeff_ref, own_ref, other_ref, base_ref, bt_ref, a_ref, mine_ref, theirs_ref, sum_ref
):
    dp, core = place_ref[0], place_ref[1]
    members = got_ref.shape[0]
    shards = members // 2
    rank = a_ref.shape[1]
    owned = 2 * own_ref.shape[0] // shards
    half = owned // 2
    at_back = got_ref.shape[1] - owned
    backs = []
    lane = lax.broadcasted_iota(jnp.int32, (1, 2 * rank), 1)
    for j in range(shards):
        source = dp * shards + j
        peaks = got_ref[source, at_back - 48 : at_back - 32, :].astype(F32)
        peak = jnp.where(lane < rank, peaks[10:11, 0:1], peaks[11:12, 0:1])
        backs.append(decode(got_ref[source, at_back:, :], peak))
    total = None
    for side, ref in enumerate((own_ref, other_ref)):
        back = jnp.concatenate([b[side * half : (side + 1) * half] for b in backs], axis=0)
        hi, lo = split(back)
        both = dot(jnp.concatenate([hi, lo], axis=1), ref[...], TN)
        part = both[: 2 * rank] + both[2 * rank :]
        total = part if total is None else total + part
    sum_ref[...] = total
    a = a_ref[dp]
    hi, lo = split(a.astype(F32) * coeff_ref[pl.ds(dp, 1), :])
    weighted = jnp.concatenate([hi, lo], axis=0)
    both = dot(weighted, base_ref[dp], NT)
    small = dot(weighted, a, NT)
    small_hi, small_lo = split(small[:rank] + small[rank:])
    value = (both[:rank] + both[rank:]) + (dot(small_hi, bt_ref[dp]) + dot(small_lo, bt_ref[dp]))
    mine = pl.ds(pl.multiple_of(dp * rank, rank), rank)
    sum_ref[mine, :] += value
    width = mine_ref.shape[1]
    mine_ref[...] = sum_ref[:, pl.ds(pl.multiple_of(core * width, width), width)]
    theirs_ref[...] = sum_ref[:, pl.ds(pl.multiple_of((1 - core) * width, width), width)]


def call(kernel, outs, in_specs, flops=0, size=0, scratch=()):
    return pl.pallas_call(
        kernel,
        out_shape=outs,
        in_specs=in_specs,
        out_specs=[VMEM] * len(outs) if isinstance(outs, (list, tuple)) else VMEM,
        scratch_shapes=scratch,
        compiler_params=PARAMS,
        cost_estimate=pl.CostEstimate(flops=flops, bytes_accessed=size, transcendentals=0),
    )


def shape(dims, dtype=F32):
    return jax.ShapeDtypeStruct(dims, dtype)


def per_device(tokens, base, b, a, magnitude, cotangent):
    dp = lax.axis_index("dp")
    core = lax.axis_index("core")
    depth, columns = base.shape[1:]
    rank = a.shape[1]
    shards = lax.axis_size("tensor")
    members = 2 * shards
    zs = lax.axis_size("z")
    own = 2 * zs * tokens.shape[0] // shards
    rows = 2 * rank // members
    tiles = columns // 128
    swap = [(0, 1), (1, 0)]
    bt = jnp.swapaxes(b, 1, 2)
    place = jnp.stack([dp, core]).astype(jnp.int32)

    g_own = lax.all_gather(tokens, "z", axis=0, tiled=True)
    g_other = lax.ppermute(g_own, "core", swap)
    cross, extra = call(
        weights_kernel,
        [shape((2 * rank, columns)), shape((48, 128))],
        [VMEM] * 3,
        flops=2 * 2 * depth * columns * rank * 3,
        size=4 * 2**20,
    )(base, bt, a)
    payload = call(
        forward_kernel,
        shape((shards, own, 2 * columns + 4 * rank), BF16),
        [VMEM] * 5,
        flops=2 * shards * own * depth * 2 * (columns + rank),
        size=8 * 2**20,
    )(g_own, g_other, base, bt.reshape(2 * rank, depth), extra)
    payload, place = lax.optimization_barrier((payload, place))
    got = lax.all_to_all(payload, "tensor", 0, 0)

    height = rows * (tiles + tiles // 2 + 1) + 32 + own
    sends, norm = call(
        local_kernel,
        [shape((members, height, 128), BF16), shape((2, columns))],
        [SMEM] + [VMEM] * 5,
        flops=2**27,
        size=4 * 2**20,
    )(place, got, cotangent, a, magnitude, cross)
    got = lax.all_to_all(sends, GROUP, 0, 0)

    a_rows, grad_m, coeff = call(
        coefficient_kernel,
        [shape((members, rows, columns)), shape((2, columns)), shape((2, columns))],
        [SMEM] + [VMEM] * 3,
        size=2 * 2**20,
    )(place, got, norm, magnitude)
    mine, theirs = call(
        width_kernel,
        [shape((2 * rank, depth // 2))] * 2,
        [SMEM] + [VMEM] * 7,
        flops=2**30,
        size=8 * 2**20,
        scratch=[pltpu.VMEM((2 * rank, depth), F32)],
    )(place, got, coeff, g_own, g_other, base, bt, a)

    part = mine + lax.ppermute(theirs, "core", swap)
    chunks = part.reshape(zs, 2 * rank // zs, depth // 2)
    piece = jnp.sum(lax.all_to_all(chunks, "z", 0, 0), axis=0)
    piece, a_rows = lax.optimization_barrier((piece, a_rows))
    grad_a = lax.all_to_all(a_rows, GROUP, 0, 0).reshape(2, rank, columns)
    piece = piece + lax.ppermute(piece, "dp", swap)
    piece, grad_a = lax.optimization_barrier((piece, grad_a))
    full = lax.all_to_all(jnp.broadcast_to(piece[None], chunks.shape), "z", 0, 0)
    full = full.reshape(2 * rank, depth // 2)
    other = lax.ppermute(full, "core", swap)
    grad_b = jnp.where(
        place[1] == 0, jnp.concatenate([full, other], axis=1), jnp.concatenate([other, full], axis=1)
    )
    return grad_a, jnp.swapaxes(grad_b.reshape(2, rank, depth), 1, 2), grad_m


def solution(mesh):
    sizes = mesh.shape
    fine = Mesh(
        mesh.devices.reshape(sizes["dp"], sizes["fsdp"] // 2, 2, sizes["tensor"]),
        ("dp", "z", "core", "tensor"),
    )
    fsdp = ("z", "core")
    return jax.shard_map(
        per_device,
        mesh=fine,
        in_specs=(
            P(("dp",) + fsdp, "tensor"),
            P(None, "tensor", fsdp),
            P(None, "tensor", None),
            P(None, None, fsdp),
            P(None, fsdp),
            P(GROUP, fsdp),
        ),
        out_specs=(P(None, None, fsdp), P(None, "tensor", None), P(None, fsdp)),
        check_vma=False,
    )
```

```python
import math

import jax
import jax.numpy as jnp
from jax import lax
from jax.experimental import pallas as pl
from jax.experimental.pallas import tpu as pltpu
from jax.sharding import Mesh, PartitionSpec as P

F32 = jnp.float32
BF16 = jnp.bfloat16
WIDTH = ("x", "y")
GROUP = ("x", "y", "dp")
PARAMS = pltpu.CompilerParams(vmem_limit_bytes=24 * 2**20)
VMEM = pl.BlockSpec(memory_space=pltpu.VMEM)
SMEM = pl.BlockSpec(memory_space=pltpu.SMEM)

BEND = 4096.0
POWER = 250.0 / math.log2(1.0 + BEND)
SHIFT = 125.0 * math.log(2.0)


def encode(x, peak):
    size = jnp.exp(POWER * jnp.log(1.0 + jnp.abs(x) * (BEND / peak)) - SHIFT)
    return jnp.where(x < 0, -size, size)


def decode(code, peak):
    code = code.astype(F32)
    size = (jnp.exp((jnp.log(jnp.abs(code)) + SHIFT) * (1.0 / POWER)) - 1.0) * (peak / BEND)
    return jnp.where(code < 0, -size, size)


def peak_of(x):
    peak = jnp.max(jnp.max(jnp.abs(x), axis=1, keepdims=True), axis=0, keepdims=True)
    return (jnp.maximum(peak, 1e-20) * 1.01).astype(BF16).astype(F32)


def split(x):
    hi = x.astype(BF16)
    return hi, (x - hi.astype(F32)).astype(BF16)


def member_of(owner):
    y, x = divmod(owner, 4)
    return x * 2 + y


def dot(x, y, dims=((1,), (0,))):
    return lax.dot_general(x, y, (dims, ((), ())), preferred_element_type=F32)


NT = ((1,), (1,))
TN = ((0,), (0,))


def weights_kernel(base_ref, bt_ref, a_ref, cross_ref, extra_ref):
    depth, columns = base_ref.shape[1:]
    rank = a_ref.shape[1]
    tiles = columns // 128
    step = 256
    extra_ref[...] = jnp.zeros_like(extra_ref)
    for k in range(2):
        sq = jnp.zeros((1, columns), F32)
        cross = jnp.zeros((rank, columns), F32)
        for at in range(0, depth, step):
            rows = slice(at, at + step)
            bt = bt_ref[k, :, rows]
            combined = base_ref[k, rows, :].astype(F32) + dot(bt, a_ref[k], TN)
            sq += jnp.sum(combined * combined, axis=0, keepdims=True)
            hi, lo = split(combined)
            cross += dot(bt, hi) + dot(bt, lo)
        cross_ref[k * rank : (k + 1) * rank, :] = cross
        for piece in range(3):
            part = sq.astype(BF16).astype(F32)
            sq = sq - part
            for i in range(tiles):
                row = 2 * tiles * piece + tiles * k + i
                extra_ref[row : row + 1, :] = part[:, 128 * i : 128 * (i + 1)]


def forward_kernel(own_ref, other_ref, base_ref, bt_ref, extra_ref, out_ref):
    shards, owned, _ = out_ref.shape
    columns = base_ref.shape[2]
    half = owned // 2
    rank = bt_ref.shape[0]
    peaks = jnp.zeros((16, 128), F32)
    line = lax.broadcasted_iota(jnp.int32, (16, 128), 0)
    row = 0
    for side, ref in enumerate((own_ref, other_ref)):
        where = slice(side * half, (side + 1) * half)
        for k in range(3):
            if k < 2:
                value = dot(ref[...], base_ref[k])
                lanes = slice(k * columns, (k + 1) * columns)
            else:
                value = dot(ref[...], bt_ref[...], NT)
                lanes = slice(2 * columns, 2 * columns + rank)
            peak = peak_of(value)
            code = encode(value, peak).astype(BF16)
            for owner in range(shards):
                out_ref[member_of(owner), where, lanes] = code[half * owner : half * (owner + 1)]
            peaks = jnp.where(line == row, peak, peaks)
            row += 1
    tail = jnp.concatenate([extra_ref[...], peaks], axis=0).astype(BF16)
    out_ref[:, :, 2 * columns + rank :] = jnp.broadcast_to(tail[None], (shards,) + tail.shape)


def local_kernel(place_ref, got_ref, cot_ref, a_ref, mag_ref, cross_ref, out_ref, norm_ref):
    dp, core = place_ref[0], place_ref[1]
    shards, owned, _ = got_ref.shape
    rank, columns = a_ref.shape[1:]
    tiles = columns // 128
    half = owned // 2
    tail = 2 * columns + 2 * rank
    peak_rows = 3 * 2 * tiles + 12

    totals = []
    for k in range(3):
        lanes = slice(k * columns, (k + 1) * columns) if k < 2 else slice(2 * columns, tail)
        sides = []
        for side in range(2):
            total = None
            for source in range(shards):
                peaks = got_ref[source, peak_rows : peak_rows + 16, tail:].astype(F32)
                at = 3 * side + k
                value = decode(
                    got_ref[source, side * half : (side + 1) * half, lanes],
                    peaks[at : at + 1, 0:1],
                )
                total = value if total is None else total + value
            sides.append(total)
        totals.append(jnp.concatenate(sides, axis=0))
    extra = got_ref[0, :48, tail:].astype(F32)
    for source in range(1, shards):
        extra += got_ref[source, :48, tail:].astype(F32)
    pieces = extra[24:36] + extra[12:24] + extra[0:12]

    low = totals[2]
    low_hi, low_lo = split(low)
    outs, pres, scales = [], [], []
    for k in range(2):
        sq = jnp.concatenate(
            [pieces[tiles * k + i : tiles * k + i + 1] for i in range(tiles)], axis=1
        )
        norm = jnp.sqrt(sq + 1e-06)
        norm_ref[k : k + 1, :] = norm
        mine = slice(k * rank, (k + 1) * rank)
        pre = totals[k] + (dot(low_hi[:, mine], a_ref[k]) + dot(low_lo[:, mine], a_ref[k]))
        scale = mag_ref[k : k + 1, :] / norm
        pres.append(pre)
        scales.append(scale)
        outs.append(pre * scale)
    gate, up = outs
    quarter = half // 2
    cot = jnp.concatenate(
        [
            cot_ref[pl.ds(pl.multiple_of(start + side * quarter, quarter), quarter), :]
            for side in (core, 1 - core)
            for start in (0, half)
        ],
        axis=0,
    ).astype(F32)
    sig = 1.0 / (1.0 + jnp.exp(-gate))
    douts = (cot * up * sig * (1.0 + gate * (1.0 - sig)), cot * gate * sig)
    members = out_ref.shape[0]
    rows = 2 * rank // members
    line = lax.broadcasted_iota(jnp.int32, (rows, 128), 0)
    codes, peaks, back_codes, back_peaks, ms = [], [], [], [], []
    for k in range(2):
        mine = slice(k * rank, (k + 1) * rank)
        ms.append(jnp.sum(douts[k] * pres[k], axis=0, keepdims=True))
        hi, lo = split(douts[k] * scales[k])
        grad_a = (
            dot(low_hi[:, mine], hi, TN) + dot(low_hi[:, mine], lo, TN) + dot(low_lo[:, mine], hi, TN)
        )
        back = dot(hi, a_ref[k], NT) + dot(lo, a_ref[k], NT)
        width = columns // 2
        cross = cross_ref[mine, pl.ds(pl.multiple_of(dp * width, width), width)]
        peaks.append((peak_of(grad_a), peak_of(cross)))
        codes.append((encode(grad_a, peaks[k][0]), encode(cross, peaks[k][1])))
        back_peaks.append(peak_of(back))
        back_codes.append(encode(back, back_peaks[k]))
    for j in range(members):
        k, at = divmod(j * rows, rank)
        blocks = [
            code[at : at + rows, 128 * i : 128 * (i + 1)]
            for code in codes[k]
            for i in range(code.shape[1] // 128)
        ]
        tail_block = jnp.zeros((rows, 128), F32)
        for row, peak in enumerate(peaks[k] + tuple(back_peaks)):
            tail_block = jnp.where(line == row, peak, tail_block)
        blocks.append(tail_block)
        for i in range(0, len(blocks), 2):
            pair = jnp.concatenate(blocks[i : i + 2], axis=0).astype(BF16)
            out_ref[j, rows * i : rows * (i + 2), :] = pair
    height = rows * (tiles + tiles // 2 + 1)
    lines = []
    for piece in range(2):
        for k in range(2):
            part = ms[k].astype(BF16).astype(F32)
            ms[k] = ms[k] - part
            lines += [part[:, 128 * i : 128 * (i + 1)] for i in range(tiles)]
    lines.append(jnp.zeros((32 - len(lines), 128), F32))
    rest = jnp.concatenate(lines + [jnp.concatenate(back_codes, axis=1)], axis=0).astype(BF16)
    out_ref[:, height:, :] = jnp.broadcast_to(rest[None], (members,) + rest.shape)


def coefficient_kernel(place_ref, got_ref, norm_ref, mag_ref, rows_ref, grad_m_ref, coeff_ref):
    members, rows, columns = rows_ref.shape
    tiles = columns // 128
    height = rows * (tiles + tiles // 2 + 1)
    m = jnp.sum(got_ref[:, height : height + 32, :].astype(F32), axis=0)
    m = m[: 2 * tiles] + m[2 * tiles : 4 * tiles]
    for k in range(2):
        norm = norm_ref[k : k + 1, :]
        m_row = jnp.concatenate([m[tiles * k + i : tiles * k + i + 1] for i in range(tiles)], axis=1)
        grad_m = m_row / norm
        grad_m_ref[k : k + 1, :] = grad_m
        coeff_ref[k : k + 1, :] = -grad_m * mag_ref[k : k + 1, :] / (norm * norm)
    coeff = jnp.where(place_ref[2] < 2, coeff_ref[0:1, :], coeff_ref[1:2, :])
    tokens = [jnp.zeros((rows, 128), F32)] * tiles
    crosses = [jnp.zeros((rows, 128), F32)] * tiles
    for j in range(members):
        blocks = got_ref[j, :height, :].astype(F32)
        peaks = blocks[height - rows :]
        token = decode(blocks[: rows * tiles], peaks[0:1, 0:1])
        cross = decode(blocks[rows * tiles : height - rows], peaks[1:2, 0:1])
        for i in range(tiles):
            tokens[i] = tokens[i] + token[rows * i : rows * (i + 1)]
        first = j % 2 * (tiles // 2)
        for i in range(tiles // 2):
            crosses[first + i] = crosses[first + i] + cross[rows * i : rows * (i + 1)]
    for i in range(tiles):
        lanes = slice(128 * i, 128 * (i + 1))
        own = tokens[i] + crosses[i] * coeff[:, lanes]
        rows_ref[:, :, lanes] = jnp.broadcast_to(own[None], (members, rows, 128))


def width_kernel(
    place_ref, got_ref, coeff_ref, own_ref, other_ref, base_ref, bt_ref, a_ref, mine_ref, theirs_ref, sum_ref
):
    dp, core = place_ref[0], place_ref[1]
    members = got_ref.shape[0]
    shards = members // 2
    rank = a_ref.shape[1]
    owned = 2 * own_ref.shape[0] // shards
    half = owned // 2
    at_back = got_ref.shape[1] - owned
    backs = []
    lane = lax.broadcasted_iota(jnp.int32, (1, 2 * rank), 1)
    for j in range(shards):
        source = member_of(j) * 2 + dp
        peaks = got_ref[source, at_back - 48 : at_back - 32, :].astype(F32)
        peak = jnp.where(lane < rank, peaks[10:11, 0:1], peaks[11:12, 0:1])
        backs.append(decode(got_ref[source, at_back:, :], peak))
    total = None
    for side, ref in enumerate((own_ref, other_ref)):
        back = jnp.concatenate([b[side * half : (side + 1) * half] for b in backs], axis=0)
        hi, lo = split(back)
        both = dot(jnp.concatenate([hi, lo], axis=1), ref[...], TN)
        part = both[: 2 * rank] + both[2 * rank :]
        total = part if total is None else total + part
    sum_ref[...] = total
    a = a_ref[dp]
    hi, lo = split(a.astype(F32) * coeff_ref[pl.ds(dp, 1), :])
    weighted = jnp.concatenate([hi, lo], axis=0)
    both = dot(weighted, base_ref[dp], NT)
    small = dot(weighted, a, NT)
    small_hi, small_lo = split(small[:rank] + small[rank:])
    value = (both[:rank] + both[rank:]) + (dot(small_hi, bt_ref[dp]) + dot(small_lo, bt_ref[dp]))
    mine = pl.ds(pl.multiple_of(dp * rank, rank), rank)
    sum_ref[mine, :] += value
    width = mine_ref.shape[1]
    mine_ref[...] = sum_ref[:, pl.ds(pl.multiple_of(core * width, width), width)]
    theirs_ref[...] = sum_ref[:, pl.ds(pl.multiple_of((1 - core) * width, width), width)]


def sum_kernel(mine_ref, theirs_ref, out_ref):
    zs, rows, lanes = out_ref.shape
    part = mine_ref[...] + theirs_ref[...]
    peak = peak_of(part)
    out_ref[:, :, : lanes - 128] = encode(part, peak).reshape(zs, rows, lanes - 128).astype(BF16)
    out_ref[:, :, lanes - 128 :] = jnp.broadcast_to(peak, (zs, rows, 128)).astype(BF16)


def decoded(got_ref):
    lanes = got_ref.shape[2] - 128
    peaks = got_ref[:, :, lanes:].astype(F32)
    return decode(got_ref[:, :, :lanes], peaks[:, 0:1, 0:1])


def piece_kernel(got_ref, out_ref):
    out_ref[...] = jnp.sum(decoded(got_ref), axis=0)


def spread_kernel(mine_ref, theirs_ref, out_ref):
    zs, rows, lanes = out_ref.shape
    piece = mine_ref[...] + theirs_ref[...]
    peak = peak_of(piece)
    code = jnp.concatenate([encode(piece, peak), jnp.broadcast_to(peak, (rows, 128))], axis=1)
    out_ref[...] = jnp.broadcast_to(code[None], (zs, rows, lanes)).astype(BF16)


def last_kernel(place_ref, own_ref, other_ref, rows_ref, grad_a_ref, grad_b_ref):
    core = place_ref[1]
    grad_a_ref[...] = rows_ref[...]
    rows, columns = grad_b_ref.shape
    width = columns // 2
    for side, ref in ((core, own_ref), (1 - core, other_ref)):
        lanes = pl.ds(pl.multiple_of(side * width, width), width)
        grad_b_ref[:, lanes] = decoded(ref).reshape(rows, width)


def call(kernel, outs, in_specs, flops=0, size=0, scratch=()):
    return pl.pallas_call(
        kernel,
        out_shape=outs,
        in_specs=in_specs,
        out_specs=[VMEM] * len(outs) if isinstance(outs, (list, tuple)) else VMEM,
        scratch_shapes=scratch,
        compiler_params=PARAMS,
        cost_estimate=pl.CostEstimate(flops=flops, bytes_accessed=size, transcendentals=0),
    )


def shape(dims, dtype=F32):
    return jax.ShapeDtypeStruct(dims, dtype)


def per_device(tokens, base, b, a, magnitude, cotangent):
    dp = lax.axis_index("dp")
    core = lax.axis_index("core")
    depth, columns = base.shape[1:]
    rank = a.shape[1]
    shards = lax.axis_size(WIDTH)
    members = 2 * shards
    zs = lax.axis_size("z")
    own = 2 * zs * tokens.shape[0] // shards
    rows = 2 * rank // members
    tiles = columns // 128
    swap = [(0, 1), (1, 0)]
    bt = jnp.swapaxes(b, 1, 2)
    place = jnp.stack([dp, core, lax.axis_index("x")]).astype(jnp.int32)

    g_own = lax.all_gather(tokens, "z", axis=0, tiled=True)
    g_other = lax.ppermute(g_own, "core", swap)
    cross, extra = call(
        weights_kernel,
        [shape((2 * rank, columns)), shape((48, 128))],
        [VMEM] * 3,
        flops=2 * 2 * depth * columns * rank * 3,
        size=4 * 2**20,
    )(base, bt, a)
    payload = call(
        forward_kernel,
        shape((shards, own, 2 * columns + 4 * rank), BF16),
        [VMEM] * 5,
        flops=2 * shards * own * depth * 2 * (columns + rank),
        size=8 * 2**20,
    )(g_own, g_other, base, bt.reshape(2 * rank, depth), extra)
    payload, place = lax.optimization_barrier((payload, place))
    got = lax.all_to_all(payload, WIDTH, 0, 0)

    height = rows * (tiles + tiles // 2 + 1) + 32 + own
    sends, norm = call(
        local_kernel,
        [shape((members, height, 128), BF16), shape((2, columns))],
        [SMEM] + [VMEM] * 5,
        flops=2**27,
        size=4 * 2**20,
    )(place, got, cotangent, a, magnitude, cross)
    got = lax.all_to_all(sends, GROUP, 0, 0)

    a_rows, grad_m, coeff = call(
        coefficient_kernel,
        [shape((members, rows, columns)), shape((2, columns)), shape((2, columns))],
        [SMEM] + [VMEM] * 3,
        size=2 * 2**20,
    )(place, got, norm, magnitude)
    mine, theirs = call(
        width_kernel,
        [shape((2 * rank, depth // 2))] * 2,
        [SMEM] + [VMEM] * 7,
        flops=2**30,
        size=8 * 2**20,
        scratch=[pltpu.VMEM((2 * rank, depth), F32)],
    )(place, got, coeff, g_own, g_other, base, bt, a)

    theirs = lax.ppermute(theirs, "core", swap)
    dims = (zs, 2 * rank // zs, depth // 2 + 128)
    chunks = call(sum_kernel, shape(dims, BF16), [VMEM] * 2, size=2**20)(mine, theirs)
    got = lax.all_to_all(chunks, "z", 0, 0)
    piece = call(piece_kernel, shape((dims[1], depth // 2)), [VMEM], size=2**18)(got)
    piece, a_rows = lax.optimization_barrier((piece, a_rows))
    grad_a = lax.all_to_all(a_rows, GROUP, 0, 0).reshape(2 * rank, columns)
    theirs = lax.ppermute(piece, "dp", swap)
    chunks = call(spread_kernel, shape(dims, BF16), [VMEM] * 2, size=2**18)(piece, theirs)
    chunks, grad_a = lax.optimization_barrier((chunks, grad_a))
    full = lax.all_to_all(chunks, "z", 0, 0)
    other = lax.ppermute(full, "core", swap)
    grad_a, grad_b = call(
        last_kernel,
        [shape((2 * rank, columns)), shape((2 * rank, depth))],
        [SMEM] + [VMEM] * 3,
        size=2**21,
    )(place, full, other, grad_a)
    grad_b = jnp.swapaxes(grad_b.reshape(2, rank, depth), 1, 2)
    return grad_a.reshape(2, rank, columns), grad_b, grad_m


def solution(mesh):
    sizes = mesh.shape
    fine = Mesh(
        mesh.devices.reshape(sizes["dp"], sizes["fsdp"] // 2, 2, 2, sizes["tensor"] // 2),
        ("dp", "z", "core", "y", "x"),
    )
    fsdp, tensor = ("z", "core"), ("y", "x")
    return jax.shard_map(
        per_device,
        mesh=fine,
        in_specs=(
            P(("dp",) + fsdp, tensor),
            P(None, tensor, fsdp),
            P(None, tensor, None),
            P(None, None, fsdp),
            P(None, fsdp),
            P(("dp",) + tensor, fsdp),
        ),
        out_specs=(P(None, None, fsdp), P(None, tensor, None), P(None, fsdp)),
        check_vma=False,
    )
```

```python
import math

import jax
import jax.numpy as jnp
from jax import lax
from jax.experimental import pallas as pl
from jax.experimental.pallas import tpu as pltpu
from jax.sharding import Mesh, PartitionSpec as P

F32 = jnp.float32
BF16 = jnp.bfloat16
WIDTH = ("x", "y")
GROUP = ("x", "y", "dp")
PARAMS = pltpu.CompilerParams(vmem_limit_bytes=24 * 2**20)
VMEM = pl.BlockSpec(memory_space=pltpu.VMEM)
SMEM = pl.BlockSpec(memory_space=pltpu.SMEM)

BEND = 4096.0
POWER = 250.0 / math.log2(1.0 + BEND)
SHIFT = 125.0 * math.log(2.0)


def encode(x, peak):
    size = jnp.exp(POWER * jnp.log(1.0 + jnp.abs(x) * (BEND / peak)) - SHIFT)
    return jnp.where(x < 0, -size, size)


def decode(code, peak):
    code = code.astype(F32)
    size = (jnp.exp((jnp.log(jnp.abs(code)) + SHIFT) * (1.0 / POWER)) - 1.0) * (peak / BEND)
    return jnp.where(code < 0, -size, size)


def peak_of(x):
    peak = jnp.max(jnp.max(jnp.abs(x), axis=1, keepdims=True), axis=0, keepdims=True)
    return (jnp.maximum(peak, 1e-20) * 1.01).astype(BF16).astype(F32)


def split(x):
    hi = x.astype(BF16)
    return hi, (x - hi.astype(F32)).astype(BF16)


def member_of(owner):
    y, x = divmod(owner, 4)
    return x * 2 + y


def dot(x, y, dims=((1,), (0,))):
    return lax.dot_general(x, y, (dims, ((), ())), preferred_element_type=F32)


NT = ((1,), (1,))
TN = ((0,), (0,))


def weights_kernel(base_ref, bt_ref, a_ref, cross_ref, extra_ref):
    depth, columns = base_ref.shape[1:]
    rank = a_ref.shape[1]
    tiles = columns // 128
    step = 256
    for k in range(2):
        sq = jnp.zeros((1, columns), F32)
        cross = jnp.zeros((rank, columns), F32)
        for at in range(0, depth, step):
            rows = slice(at, at + step)
            bt = bt_ref[k, :, rows]
            combined = base_ref[k, rows, :].astype(F32) + dot(bt, a_ref[k], TN)
            sq += jnp.sum(combined * combined, axis=0, keepdims=True)
            hi, lo = split(combined)
            cross += dot(bt, hi) + dot(bt, lo)
        cross_ref[k * rank : (k + 1) * rank, :] = cross
        for piece in range(2):
            part = sq.astype(BF16).astype(F32)
            sq = sq - part
            for i in range(tiles):
                row = 2 * tiles * piece + tiles * k + i
                extra_ref[row : row + 1, :] = part[:, 128 * i : 128 * (i + 1)]


def forward_kernel(own_ref, other_ref, base_ref, bt_ref, extra_ref, out_ref):
    shards = out_ref.shape[0]
    columns = base_ref.shape[2]
    half = own_ref.shape[0] // shards
    owned = 2 * half
    tiles = columns // 128
    peaks = jnp.zeros((8, 128), F32)
    line = lax.broadcasted_iota(jnp.int32, (8, 128), 0)
    for side, ref in enumerate((own_ref, other_ref)):
        for k in range(3):
            value = dot(ref[...], base_ref[k]) if k < 2 else dot(ref[...], bt_ref[...], NT)
            peak = peak_of(value)
            code = encode(value, peak).astype(BF16)
            for owner in range(shards):
                for i in range(value.shape[1] // 128):
                    at = (tiles * k + i) * owned + side * half
                    out_ref[member_of(owner), at : at + half, :] = code[
                        half * owner : half * (owner + 1), 128 * i : 128 * (i + 1)
                    ]
            peaks = jnp.where(line == 3 * side + k, peak, peaks)
    rest = jnp.concatenate([extra_ref[...], peaks], axis=0).astype(BF16)
    out_ref[:, (2 * tiles + 1) * owned :, :] = jnp.broadcast_to(rest[None], (shards,) + rest.shape)


def local_kernel(place_ref, got_ref, cot_ref, a_ref, mag_ref, cross_ref, out_ref, norm_ref):
    dp, core = place_ref[0], place_ref[1]
    shards = got_ref.shape[0]
    rank, columns = a_ref.shape[1:]
    owned = cot_ref.shape[0]
    tiles = columns // 128
    half = owned // 2
    at_extra = (2 * tiles + 1) * owned

    rests = [got_ref[source, at_extra:, :].astype(F32) for source in range(shards)]
    totals = []
    for k in range(3):
        sides = []
        for side in range(2):
            row = 4 * tiles + 3 * side + k
            parts = []
            for i in range(tiles if k < 2 else 1):
                at = (tiles * k + i) * owned + side * half
                total = None
                for source in range(shards):
                    value = decode(
                        got_ref[source, at : at + half, :], rests[source][row : row + 1, 0:1]
                    )
                    total = value if total is None else total + value
                parts.append(total)
            sides.append(jnp.concatenate(parts, axis=1) if k < 2 else parts[0])
        totals.append(jnp.concatenate(sides, axis=0))
    extra = rests[0]
    for source in range(1, shards):
        extra = extra + rests[source]
    pieces = extra[2 * tiles : 4 * tiles] + extra[: 2 * tiles]

    low = totals[2]
    low_hi, low_lo = split(low)
    outs, pres, scales = [], [], []
    for k in range(2):
        sq = jnp.concatenate(
            [pieces[tiles * k + i : tiles * k + i + 1] for i in range(tiles)], axis=1
        )
        norm = jnp.sqrt(sq + 1e-06)
        norm_ref[k : k + 1, :] = norm
        mine = slice(k * rank, (k + 1) * rank)
        pre = totals[k] + (dot(low_hi[:, mine], a_ref[k]) + dot(low_lo[:, mine], a_ref[k]))
        scale = mag_ref[k : k + 1, :] / norm
        pres.append(pre)
        scales.append(scale)
        outs.append(pre * scale)
    gate, up = outs
    quarter = half // 2
    cot = jnp.concatenate(
        [
            cot_ref[pl.ds(pl.multiple_of(start + side * quarter, quarter), quarter), :]
            for side in (core, 1 - core)
            for start in (0, half)
        ],
        axis=0,
    ).astype(F32)
    sig = 1.0 / (1.0 + jnp.exp(-gate))
    douts = (cot * up * sig * (1.0 + gate * (1.0 - sig)), cot * gate * sig)
    members = out_ref.shape[0]
    rows = 2 * rank // members
    codes, peaks, back_codes, back_peaks, ms = [], [], [], [], []
    for k in range(2):
        mine = slice(k * rank, (k + 1) * rank)
        ms.append(jnp.sum(douts[k] * pres[k], axis=0, keepdims=True))
        hi, lo = split(douts[k] * scales[k])
        grad_a = (
            dot(low_hi[:, mine], hi, TN) + dot(low_hi[:, mine], lo, TN) + dot(low_lo[:, mine], hi, TN)
        )
        back = dot(hi, a_ref[k], NT) + dot(lo, a_ref[k], NT)
        width = columns // 2
        cross = cross_ref[mine, pl.ds(pl.multiple_of(dp * width, width), width)]
        peaks.append((peak_of(grad_a), peak_of(cross)))
        codes.append((encode(grad_a, peaks[k][0]), encode(cross, peaks[k][1])))
        back_peaks.append(peak_of(back))
        back_codes.append(encode(back, back_peaks[k]))
    m_peaks = [peak_of(m) for m in ms]
    m_codes = [
        encode(m, peak)[:, 128 * i : 128 * (i + 1)]
        for m, peak in zip(ms, m_peaks)
        for i in range(tiles)
    ]
    first_half = lax.broadcasted_iota(jnp.int32, (1, 128), 1) < 64
    pair = lambda x, y: jnp.where(first_half, x, y)
    ends = [pair(*back_peaks), pair(*m_peaks), jnp.zeros((1, 128), F32)]
    spare = m_codes[rows:]
    at_back = rows * (tiles + tiles // 2 + 1)
    for j in range(members):
        k, at = divmod(j * rows, rank)
        blocks = [
            code[at : at + rows, 128 * i : 128 * (i + 1)]
            for code in codes[k]
            for i in range(code.shape[1] // 128)
        ]
        blocks.append(jnp.concatenate(spare + [pair(*peaks[k])] + ends, axis=0))
        for i in range(0, len(blocks), 2):
            two = jnp.concatenate(blocks[i : i + 2], axis=0).astype(BF16)
            out_ref[j, rows * i : rows * (i + 2), :] = two
    rest = jnp.concatenate([jnp.concatenate(back_codes, axis=1)] + m_codes[:rows], axis=0).astype(BF16)
    out_ref[:, at_back:, :] = jnp.broadcast_to(rest[None], (members,) + rest.shape)


def rows_kernel(place_ref, got_ref, coeff_ref, rows_ref):
    members, rows, columns = rows_ref.shape
    tiles = columns // 128
    height = rows * (tiles + tiles // 2 + 1)
    coeff = jnp.where(place_ref[2] < 2, coeff_ref[0:1, :], coeff_ref[1:2, :])
    tokens = [jnp.zeros((rows, 128), F32)] * tiles
    crosses = [jnp.zeros((rows, 128), F32)] * tiles
    for j in range(members):
        blocks = got_ref[j, :height, :].astype(F32)
        peaks = blocks[height - 4 : height - 3]
        token = decode(blocks[: rows * tiles], peaks[:, 0:1])
        cross = decode(blocks[rows * tiles : height - rows], peaks[:, 64:65])
        for i in range(tiles):
            tokens[i] = tokens[i] + token[rows * i : rows * (i + 1)]
        first = j % 2 * (tiles // 2)
        for i in range(tiles // 2):
            crosses[first + i] = crosses[first + i] + cross[rows * i : rows * (i + 1)]
    for i in range(tiles):
        lanes = slice(128 * i, 128 * (i + 1))
        own = tokens[i] + crosses[i] * coeff[:, lanes]
        rows_ref[:, :, lanes] = jnp.broadcast_to(own[None], (members, rows, 128))


def width_kernel(
    place_ref, got_ref, norm_ref, mag_ref, own_ref, other_ref, base_ref, bt_ref, a_ref,
    mine_ref, theirs_ref, grad_m_ref, coeff_ref, sum_ref,
):
    dp, core = place_ref[0], place_ref[1]
    members = got_ref.shape[0]
    shards = members // 2
    rank, columns = a_ref.shape[1:]
    tiles = columns // 128
    owned = 2 * own_ref.shape[0] // shards
    half = owned // 2
    height = got_ref.shape[1]
    at_back = height - 8 - owned
    line = lax.broadcasted_iota(jnp.int32, (2 * tiles, 1), 0)
    m = None
    for j in range(members):
        ends = got_ref[j, at_back - 16 : at_back, :].astype(F32)[8:]
        code = jnp.concatenate([got_ref[j, height - 8 :, :].astype(F32), ends[:4]], axis=0)
        part = decode(code, jnp.where(line < tiles, ends[6:7, 0:1], ends[6:7, 64:65]))
        m = part if m is None else m + part
    for k in range(2):
        norm = norm_ref[k : k + 1, :]
        m_row = jnp.concatenate([m[tiles * k + i : tiles * k + i + 1] for i in range(tiles)], axis=1)
        grad_m = m_row / norm
        grad_m_ref[k : k + 1, :] = grad_m
        coeff_ref[k : k + 1, :] = -grad_m * mag_ref[k : k + 1, :] / (norm * norm)
    backs = []
    lane = lax.broadcasted_iota(jnp.int32, (1, 2 * rank), 1)
    for j in range(shards):
        source = member_of(j) * 2 + dp
        ends = got_ref[source, at_back - 16 : at_back, :].astype(F32)
        peak = jnp.where(lane < rank, ends[13:14, 0:1], ends[13:14, 64:65])
        backs.append(decode(got_ref[source, at_back : at_back + owned, :], peak))
    total = None
    for side, ref in enumerate((own_ref, other_ref)):
        back = jnp.concatenate([b[side * half : (side + 1) * half] for b in backs], axis=0)
        hi, lo = split(back)
        both = dot(jnp.concatenate([hi, lo], axis=1), ref[...], TN)
        part = both[: 2 * rank] + both[2 * rank :]
        total = part if total is None else total + part
    sum_ref[...] = total
    a = a_ref[dp]
    hi, lo = split(a.astype(F32) * coeff_ref[pl.ds(dp, 1), :])
    weighted = jnp.concatenate([hi, lo], axis=0)
    both = dot(weighted, base_ref[dp], NT)
    small = dot(weighted, a, NT)
    small_hi, small_lo = split(small[:rank] + small[rank:])
    value = (both[:rank] + both[rank:]) + (dot(small_hi, bt_ref[dp]) + dot(small_lo, bt_ref[dp]))
    mine = pl.ds(pl.multiple_of(dp * rank, rank), rank)
    sum_ref[mine, :] += value
    width = mine_ref.shape[1]
    mine_ref[...] = sum_ref[:, pl.ds(pl.multiple_of(core * width, width), width)]
    theirs_ref[...] = sum_ref[:, pl.ds(pl.multiple_of((1 - core) * width, width), width)]


def sum_kernel(mine_ref, theirs_ref, out_ref):
    zs, rows, lanes = out_ref.shape
    part = mine_ref[...] + theirs_ref[...]
    peak = peak_of(part)
    out_ref[:, :, : lanes - 128] = encode(part, peak).reshape(zs, rows, lanes - 128).astype(BF16)
    out_ref[:, :, lanes - 128 :] = jnp.broadcast_to(peak, (zs, rows, 128)).astype(BF16)


def decoded(got_ref):
    lanes = got_ref.shape[2] - 128
    peaks = got_ref[:, :, lanes:].astype(F32)
    return decode(got_ref[:, :, :lanes], peaks[:, 0:1, 0:1])


def piece_kernel(got_ref, out_ref):
    out_ref[...] = jnp.sum(decoded(got_ref), axis=0)


def spread_kernel(mine_ref, theirs_ref, out_ref):
    zs, rows, lanes = out_ref.shape
    piece = mine_ref[...] + theirs_ref[...]
    peak = peak_of(piece)
    code = jnp.concatenate([encode(piece, peak), jnp.broadcast_to(peak, (rows, 128))], axis=1)
    out_ref[...] = jnp.broadcast_to(code[None], (zs, rows, lanes)).astype(BF16)


def last_kernel(place_ref, own_ref, other_ref, rows_ref, grad_a_ref, grad_b_ref):
    core = place_ref[1]
    grad_a_ref[...] = rows_ref[...]
    rows, columns = grad_b_ref.shape
    width = columns // 2
    for side, ref in ((core, own_ref), (1 - core, other_ref)):
        lanes = pl.ds(pl.multiple_of(side * width, width), width)
        grad_b_ref[:, lanes] = decoded(ref).reshape(rows, width)


def call(kernel, outs, in_specs, flops=0, size=0, scratch=()):
    return pl.pallas_call(
        kernel,
        out_shape=outs,
        in_specs=in_specs,
        out_specs=[VMEM] * len(outs) if isinstance(outs, (list, tuple)) else VMEM,
        scratch_shapes=scratch,
        compiler_params=PARAMS,
        cost_estimate=pl.CostEstimate(flops=flops, bytes_accessed=size, transcendentals=0),
    )


def shape(dims, dtype=F32):
    return jax.ShapeDtypeStruct(dims, dtype)


def per_device(tokens, base, b, a, magnitude, cotangent):
    dp = lax.axis_index("dp")
    core = lax.axis_index("core")
    depth, columns = base.shape[1:]
    rank = a.shape[1]
    shards = lax.axis_size(WIDTH)
    members = 2 * shards
    zs = lax.axis_size("z")
    own = 2 * zs * tokens.shape[0] // shards
    rows = 2 * rank // members
    tiles = columns // 128
    swap = [(0, 1), (1, 0)]
    bt = jnp.swapaxes(b, 1, 2)
    place = jnp.stack([dp, core, lax.axis_index("x")]).astype(jnp.int32)

    g_own = lax.all_gather(tokens, "z", axis=0, tiled=True)
    g_other = lax.ppermute(g_own, "core", swap)
    cross, extra = call(
        weights_kernel,
        [shape((2 * rank, columns)), shape((4 * tiles, 128))],
        [VMEM] * 3,
        flops=2 * 2 * depth * columns * rank * 3,
        size=4 * 2**20,
    )(base, bt, a)
    payload = call(
        forward_kernel,
        shape((shards, (2 * tiles + 1) * own + 4 * tiles + 8, 128), BF16),
        [VMEM] * 5,
        flops=2 * shards * own * depth * 2 * (columns + rank),
        size=8 * 2**20,
    )(g_own, g_other, base, bt.reshape(2 * rank, depth), extra)
    payload, place = lax.optimization_barrier((payload, place))
    got = lax.all_to_all(payload, WIDTH, 0, 0)

    height = rows * (tiles + tiles // 2 + 1) + own + 8
    sends, norm = call(
        local_kernel,
        [shape((members, height, 128), BF16), shape((2, columns))],
        [SMEM] + [VMEM] * 5,
        flops=2**27,
        size=4 * 2**20,
    )(place, got, cotangent, a, magnitude, cross)
    got = lax.all_to_all(sends, GROUP, 0, 0)

    mine, theirs, grad_m, coeff = call(
        width_kernel,
        [shape((2 * rank, depth // 2))] * 2 + [shape((2, columns))] * 2,
        [SMEM] + [VMEM] * 8,
        flops=2**30,
        size=8 * 2**20,
        scratch=[pltpu.VMEM((2 * rank, depth), F32)],
    )(place, got, norm, magnitude, g_own, g_other, base, bt, a)
    a_rows = call(
        rows_kernel,
        shape((members, rows, columns)),
        [SMEM] + [VMEM] * 2,
        flops=2**22,
        size=2**20,
    )(place, got, coeff)

    theirs = lax.ppermute(theirs, "core", swap)
    dims = (zs, 2 * rank // zs, depth // 2 + 128)
    chunks = call(sum_kernel, shape(dims, BF16), [VMEM] * 2, size=2**20)(mine, theirs)
    got = lax.all_to_all(chunks, "z", 0, 0)
    piece = call(piece_kernel, shape((dims[1], depth // 2)), [VMEM], size=2**18)(got)
    piece, a_rows = lax.optimization_barrier((piece, a_rows))
    grad_a = lax.all_to_all(a_rows, GROUP, 0, 0).reshape(2 * rank, columns)
    theirs = lax.ppermute(piece, "dp", swap)
    chunks = call(spread_kernel, shape(dims, BF16), [VMEM] * 2, size=2**18)(piece, theirs)
    chunks, grad_a = lax.optimization_barrier((chunks, grad_a))
    full = lax.all_to_all(chunks, "z", 0, 0)
    other = lax.ppermute(full, "core", swap)
    grad_a, grad_b = call(
        last_kernel,
        [shape((2 * rank, columns)), shape((2 * rank, depth))],
        [SMEM] + [VMEM] * 3,
        size=2**21,
    )(place, full, other, grad_a)
    grad_b = jnp.swapaxes(grad_b.reshape(2, rank, depth), 1, 2)
    return grad_a.reshape(2, rank, columns), grad_b, grad_m


def solution(mesh):
    sizes = mesh.shape
    fine = Mesh(
        mesh.devices.reshape(sizes["dp"], sizes["fsdp"] // 2, 2, 2, sizes["tensor"] // 2),
        ("dp", "z", "core", "y", "x"),
    )
    fsdp, tensor = ("z", "core"), ("y", "x")
    return jax.shard_map(
        per_device,
        mesh=fine,
        in_specs=(
            P(("dp",) + fsdp, tensor),
            P(None, tensor, fsdp),
            P(None, tensor, None),
            P(None, None, fsdp),
            P(None, fsdp),
            P(("dp",) + tensor, fsdp),
        ),
        out_specs=(P(None, None, fsdp), P(None, tensor, None), P(None, fsdp)),
        check_vma=False,
    )
```

```python
import math

import jax
import jax.numpy as jnp
from jax import lax
from jax.experimental import pallas as pl
from jax.experimental.pallas import tpu as pltpu
from jax.sharding import Mesh, PartitionSpec as P

F32 = jnp.float32
BF16 = jnp.bfloat16
WIDTH = ("x", "y")
GROUP = ("x", "y", "dp")
PARAMS = pltpu.CompilerParams(vmem_limit_bytes=24 * 2**20)
VMEM = pl.BlockSpec(memory_space=pltpu.VMEM)
SMEM = pl.BlockSpec(memory_space=pltpu.SMEM)

BEND = 4096.0
POWER = 250.0 / math.log2(1.0 + BEND)
SHIFT = 125.0 * math.log(2.0)


def encode(x, peak):
    size = jnp.exp(POWER * jnp.log(1.0 + jnp.abs(x) * (BEND / peak)) - SHIFT)
    return jnp.where(x < 0, -size, size)


def decode(code, peak):
    code = code.astype(F32)
    size = (jnp.exp((jnp.log(jnp.abs(code)) + SHIFT) * (1.0 / POWER)) - 1.0) * (peak / BEND)
    return jnp.where(code < 0, -size, size)


def peak_of(x):
    peak = jnp.max(jnp.max(jnp.abs(x), axis=1, keepdims=True), axis=0, keepdims=True)
    return (jnp.maximum(peak, 1e-20) * 1.01).astype(BF16).astype(F32)


def split(x):
    hi = x.astype(BF16)
    return hi, (x - hi.astype(F32)).astype(BF16)


def member_of(owner):
    y, x = divmod(owner, 4)
    return x * 2 + y


def dot(x, y, dims=((1,), (0,))):
    return lax.dot_general(x, y, (dims, ((), ())), preferred_element_type=F32)


NT = ((1,), (1,))
TN = ((0,), (0,))


def weights_kernel(base_ref, bt_ref, a_ref, cross_ref, extra_ref):
    depth, columns = base_ref.shape[1:]
    rank = a_ref.shape[1]
    tiles = columns // 128
    step = 256
    for k in range(2):
        sq = jnp.zeros((1, columns), F32)
        cross = jnp.zeros((rank, columns), F32)
        for at in range(0, depth, step):
            rows = slice(at, at + step)
            bt = bt_ref[k, :, rows]
            combined = base_ref[k, rows, :].astype(F32) + dot(bt, a_ref[k], TN)
            sq += jnp.sum(combined * combined, axis=0, keepdims=True)
            hi, lo = split(combined)
            cross += dot(bt, hi) + dot(bt, lo)
        cross_ref[k * rank : (k + 1) * rank, :] = cross
        for piece in range(2):
            part = sq.astype(BF16).astype(F32)
            sq = sq - part
            for i in range(tiles):
                row = 2 * tiles * piece + tiles * k + i
                extra_ref[row : row + 1, :] = part[:, 128 * i : 128 * (i + 1)]


def forward_kernel(own_ref, other_ref, base_ref, bt_ref, extra_ref, out_ref):
    shards = out_ref.shape[0]
    columns = base_ref.shape[2]
    half = own_ref.shape[0] // shards
    owned = 2 * half
    tiles = columns // 128
    peaks = jnp.zeros((8, 128), F32)
    line = lax.broadcasted_iota(jnp.int32, (8, 128), 0)
    for side, ref in enumerate((own_ref, other_ref)):
        for k in range(3):
            value = dot(ref[...], base_ref[k]) if k < 2 else dot(ref[...], bt_ref[...], NT)
            peak = peak_of(value)
            code = encode(value, peak).astype(BF16)
            for owner in range(shards):
                for i in range(value.shape[1] // 128):
                    at = (tiles * k + i) * owned + side * half
                    out_ref[member_of(owner), at : at + half, :] = code[
                        half * owner : half * (owner + 1), 128 * i : 128 * (i + 1)
                    ]
            peaks = jnp.where(line == 3 * side + k, peak, peaks)
    rest = jnp.concatenate([extra_ref[...], peaks], axis=0).astype(BF16)
    out_ref[:, (2 * tiles + 1) * owned :, :] = jnp.broadcast_to(rest[None], (shards,) + rest.shape)


def local_kernel(place_ref, got_ref, cot_ref, a_ref, mag_ref, cross_ref, out_ref, norm_ref):
    dp, core = place_ref[0], place_ref[1]
    shards = got_ref.shape[0]
    rank, columns = a_ref.shape[1:]
    owned = cot_ref.shape[0]
    tiles = columns // 128
    half = owned // 2
    at_extra = (2 * tiles + 1) * owned

    rests = [got_ref[source, at_extra:, :].astype(F32) for source in range(shards)]
    totals = []
    for k in range(3):
        sides = []
        for side in range(2):
            row = 4 * tiles + 3 * side + k
            parts = []
            for i in range(tiles if k < 2 else 1):
                at = (tiles * k + i) * owned + side * half
                total = None
                for source in range(shards):
                    value = decode(
                        got_ref[source, at : at + half, :], rests[source][row : row + 1, 0:1]
                    )
                    total = value if total is None else total + value
                parts.append(total)
            sides.append(jnp.concatenate(parts, axis=1) if k < 2 else parts[0])
        totals.append(jnp.concatenate(sides, axis=0))
    extra = rests[0]
    for source in range(1, shards):
        extra = extra + rests[source]
    pieces = extra[2 * tiles : 4 * tiles] + extra[: 2 * tiles]

    low = totals[2]
    low_hi, low_lo = split(low)
    outs, pres, scales = [], [], []
    for k in range(2):
        sq = jnp.concatenate(
            [pieces[tiles * k + i : tiles * k + i + 1] for i in range(tiles)], axis=1
        )
        norm = jnp.sqrt(sq + 1e-06)
        norm_ref[k : k + 1, :] = norm
        mine = slice(k * rank, (k + 1) * rank)
        pre = totals[k] + (dot(low_hi[:, mine], a_ref[k]) + dot(low_lo[:, mine], a_ref[k]))
        scale = mag_ref[k : k + 1, :] / norm
        pres.append(pre)
        scales.append(scale)
        outs.append(pre * scale)
    gate, up = outs
    quarter = half // 2
    cot = jnp.concatenate(
        [
            cot_ref[pl.ds(pl.multiple_of(start + side * quarter, quarter), quarter), :]
            for side in (core, 1 - core)
            for start in (0, half)
        ],
        axis=0,
    ).astype(F32)
    sig = 1.0 / (1.0 + jnp.exp(-gate))
    douts = (cot * up * sig * (1.0 + gate * (1.0 - sig)), cot * gate * sig)
    members = out_ref.shape[0]
    rows = 2 * rank // members
    codes, peaks, back_codes, back_peaks, ms = [], [], [], [], []
    for k in range(2):
        mine = slice(k * rank, (k + 1) * rank)
        ms.append(jnp.sum(douts[k] * pres[k], axis=0, keepdims=True))
        hi, lo = split(douts[k] * scales[k])
        grad_a = (
            dot(low_hi[:, mine], hi, TN) + dot(low_hi[:, mine], lo, TN) + dot(low_lo[:, mine], hi, TN)
        )
        back = dot(hi, a_ref[k], NT) + dot(lo, a_ref[k], NT)
        width = columns // 2
        cross = cross_ref[mine, pl.ds(pl.multiple_of(dp * width, width), width)]
        peaks.append((peak_of(grad_a), peak_of(cross)))
        codes.append((encode(grad_a, peaks[k][0]), encode(cross, peaks[k][1])))
        back_peaks.append(peak_of(back))
        back_codes.append(encode(back, back_peaks[k]))
    m_peaks = [peak_of(m) for m in ms]
    m_codes = [
        encode(m, peak)[:, 128 * i : 128 * (i + 1)]
        for m, peak in zip(ms, m_peaks)
        for i in range(tiles)
    ]
    first_half = lax.broadcasted_iota(jnp.int32, (1, 128), 1) < 64
    pair = lambda x, y: jnp.where(first_half, x, y)
    ends = [pair(*back_peaks), pair(*m_peaks), jnp.zeros((1, 128), F32)]
    spare = m_codes[rows:]
    at_back = rows * (tiles + tiles // 2 + 1)
    for j in range(members):
        k, at = divmod(j * rows, rank)
        blocks = [
            code[at : at + rows, 128 * i : 128 * (i + 1)]
            for code in codes[k]
            for i in range(code.shape[1] // 128)
        ]
        blocks.append(jnp.concatenate(spare + [pair(*peaks[k])] + ends, axis=0))
        for i in range(0, len(blocks), 2):
            two = jnp.concatenate(blocks[i : i + 2], axis=0).astype(BF16)
            out_ref[j, rows * i : rows * (i + 2), :] = two
    rest = jnp.concatenate([jnp.concatenate(back_codes, axis=1)] + m_codes[:rows], axis=0).astype(BF16)
    out_ref[:, at_back:, :] = jnp.broadcast_to(rest[None], (members,) + rest.shape)


def rows_kernel(place_ref, got_ref, coeff_ref, rows_ref):
    members = got_ref.shape[0]
    rows, columns = rows_ref.shape
    tiles = columns // 128
    height = rows * (tiles + tiles // 2 + 1)
    coeff = jnp.where(place_ref[2] < 2, coeff_ref[0:1, :], coeff_ref[1:2, :])
    tokens = [jnp.zeros((rows, 128), F32)] * tiles
    crosses = [jnp.zeros((rows, 128), F32)] * tiles
    for j in range(members):
        blocks = got_ref[j, :height, :].astype(F32)
        peaks = blocks[height - 4 : height - 3]
        token = decode(blocks[: rows * tiles], peaks[:, 0:1])
        cross = decode(blocks[rows * tiles : height - rows], peaks[:, 64:65])
        for i in range(tiles):
            tokens[i] = tokens[i] + token[rows * i : rows * (i + 1)]
        first = j % 2 * (tiles // 2)
        for i in range(tiles // 2):
            crosses[first + i] = crosses[first + i] + cross[rows * i : rows * (i + 1)]
    for i in range(tiles):
        lanes = slice(128 * i, 128 * (i + 1))
        rows_ref[:, lanes] = tokens[i] + crosses[i] * coeff[:, lanes]


def width_kernel(
    place_ref, got_ref, norm_ref, mag_ref, own_ref, other_ref, base_ref, bt_ref, a_ref,
    mine_ref, theirs_ref, grad_m_ref, coeff_ref, sum_ref,
):
    dp, core = place_ref[0], place_ref[1]
    members = got_ref.shape[0]
    shards = members // 2
    rank, columns = a_ref.shape[1:]
    tiles = columns // 128
    owned = 2 * own_ref.shape[0] // shards
    half = owned // 2
    height = got_ref.shape[1]
    at_back = height - 8 - owned
    line = lax.broadcasted_iota(jnp.int32, (2 * tiles, 1), 0)
    m = None
    for j in range(members):
        ends = got_ref[j, at_back - 16 : at_back, :].astype(F32)[8:]
        code = jnp.concatenate([got_ref[j, height - 8 :, :].astype(F32), ends[:4]], axis=0)
        part = decode(code, jnp.where(line < tiles, ends[6:7, 0:1], ends[6:7, 64:65]))
        m = part if m is None else m + part
    for k in range(2):
        norm = norm_ref[k : k + 1, :]
        m_row = jnp.concatenate([m[tiles * k + i : tiles * k + i + 1] for i in range(tiles)], axis=1)
        grad_m = m_row / norm
        grad_m_ref[k : k + 1, :] = grad_m
        coeff_ref[k : k + 1, :] = -grad_m * mag_ref[k : k + 1, :] / (norm * norm)
    backs = []
    lane = lax.broadcasted_iota(jnp.int32, (1, 2 * rank), 1)
    for j in range(shards):
        source = member_of(j) * 2 + dp
        ends = got_ref[source, at_back - 16 : at_back, :].astype(F32)
        peak = jnp.where(lane < rank, ends[13:14, 0:1], ends[13:14, 64:65])
        backs.append(decode(got_ref[source, at_back : at_back + owned, :], peak))
    total = None
    for side, ref in enumerate((own_ref, other_ref)):
        back = jnp.concatenate([b[side * half : (side + 1) * half] for b in backs], axis=0)
        hi, lo = split(back)
        both = dot(jnp.concatenate([hi, lo], axis=1), ref[...], TN)
        part = both[: 2 * rank] + both[2 * rank :]
        total = part if total is None else total + part
    sum_ref[...] = total
    a = a_ref[dp]
    hi, lo = split(a.astype(F32) * coeff_ref[pl.ds(dp, 1), :])
    weighted = jnp.concatenate([hi, lo], axis=0)
    both = dot(weighted, base_ref[dp], NT)
    small = dot(weighted, a, NT)
    small_hi, small_lo = split(small[:rank] + small[rank:])
    value = (both[:rank] + both[rank:]) + (dot(small_hi, bt_ref[dp]) + dot(small_lo, bt_ref[dp]))
    mine = pl.ds(pl.multiple_of(dp * rank, rank), rank)
    sum_ref[mine, :] += value
    width = mine_ref.shape[1]
    mine_ref[...] = sum_ref[:, pl.ds(pl.multiple_of(core * width, width), width)]
    theirs_ref[...] = sum_ref[:, pl.ds(pl.multiple_of((1 - core) * width, width), width)]


def sum_kernel(mine_ref, theirs_ref, out_ref):
    zs, rows, lanes = out_ref.shape
    part = mine_ref[...] + theirs_ref[...]
    peak = peak_of(part)
    out_ref[:, :, : lanes - 128] = encode(part, peak).reshape(zs, rows, lanes - 128).astype(BF16)
    out_ref[:, :, lanes - 128 :] = jnp.broadcast_to(peak, (zs, rows, 128)).astype(BF16)


def decoded(got_ref):
    lanes = got_ref.shape[2] - 128
    peaks = got_ref[:, :, lanes:].astype(F32)
    return decode(got_ref[:, :, :lanes], peaks[:, 0:1, 0:1])


def piece_kernel(got_ref, rows_ref, far_ref, out_ref):
    rows, width = got_ref.shape[1], got_ref.shape[2] - 128
    columns = out_ref.shape[1]
    out_ref[:rows, :width] = jnp.sum(decoded(got_ref), axis=0)
    out_ref[:rows, width:] = jnp.zeros((rows, columns - width), F32)
    out_ref[rows : 2 * rows, :] = rows_ref[...]
    out_ref[2 * rows :, :] = far_ref[...]


def spread_kernel(mine_ref, theirs_ref, out_ref, rows_ref):
    zs, rows, lanes = out_ref.shape
    width = lanes - 128
    piece = mine_ref[:rows, :width] + theirs_ref[:rows, :width]
    peak = peak_of(piece)
    code = jnp.concatenate([encode(piece, peak), jnp.broadcast_to(peak, (rows, 128))], axis=1)
    out_ref[...] = jnp.broadcast_to(code[None], (zs, rows, lanes)).astype(BF16)
    rows_ref[: 2 * rows, :] = mine_ref[rows:, :]
    rows_ref[2 * rows :, :] = theirs_ref[rows:, :]


def last_kernel(place_ref, own_ref, other_ref, r0_ref, r1_ref, r2_ref, r3_ref, grad_a_ref, grad_b_ref):
    core, member = place_ref[1], place_ref[3]
    count = own_ref.shape[1]
    for near, ref in enumerate((r0_ref, r1_ref, r2_ref, r3_ref)):
        for i, far in enumerate((0, 8, 1, 9)):
            at = pl.multiple_of(jnp.bitwise_xor(member, 2 * near + far) * count, count)
            grad_a_ref[pl.ds(at, count), :] = ref[count * i : count * (i + 1), :]
    rows, columns = grad_b_ref.shape
    width = columns // 2
    for side, ref in ((core, own_ref), (1 - core, other_ref)):
        lanes = pl.ds(pl.multiple_of(side * width, width), width)
        grad_b_ref[:, lanes] = decoded(ref).reshape(rows, width)


def call(kernel, outs, in_specs, flops=0, size=0, scratch=()):
    return pl.pallas_call(
        kernel,
        out_shape=outs,
        in_specs=in_specs,
        out_specs=[VMEM] * len(outs) if isinstance(outs, (list, tuple)) else VMEM,
        scratch_shapes=scratch,
        compiler_params=PARAMS,
        cost_estimate=pl.CostEstimate(flops=flops, bytes_accessed=size, transcendentals=0),
    )


def shape(dims, dtype=F32):
    return jax.ShapeDtypeStruct(dims, dtype)


def per_device(tokens, base, b, a, magnitude, cotangent):
    dp = lax.axis_index("dp")
    core = lax.axis_index("core")
    depth, columns = base.shape[1:]
    rank = a.shape[1]
    shards = lax.axis_size(WIDTH)
    members = 2 * shards
    zs = lax.axis_size("z")
    own = 2 * zs * tokens.shape[0] // shards
    rows = 2 * rank // members
    tiles = columns // 128
    swap = [(0, 1), (1, 0)]
    bt = jnp.swapaxes(b, 1, 2)
    place = jnp.stack([dp, core, lax.axis_index("x"), lax.axis_index(GROUP)]).astype(jnp.int32)

    g_own = lax.all_gather(tokens, "z", axis=0, tiled=True)
    g_other = lax.ppermute(g_own, "core", swap)
    cross, extra = call(
        weights_kernel,
        [shape((2 * rank, columns)), shape((4 * tiles, 128))],
        [VMEM] * 3,
        flops=2 * 2 * depth * columns * rank * 3,
        size=4 * 2**20,
    )(base, bt, a)
    payload = call(
        forward_kernel,
        shape((shards, (2 * tiles + 1) * own + 4 * tiles + 8, 128), BF16),
        [VMEM] * 5,
        flops=2 * shards * own * depth * 2 * (columns + rank),
        size=8 * 2**20,
    )(g_own, g_other, base, bt.reshape(2 * rank, depth), extra)
    payload, place = lax.optimization_barrier((payload, place))
    got = lax.all_to_all(payload, WIDTH, 0, 0)

    height = rows * (tiles + tiles // 2 + 1) + own + 8
    sends, norm = call(
        local_kernel,
        [shape((members, height, 128), BF16), shape((2, columns))],
        [SMEM] + [VMEM] * 5,
        flops=2**27,
        size=4 * 2**20,
    )(place, got, cotangent, a, magnitude, cross)
    got = lax.all_to_all(sends, GROUP, 0, 0)

    mine, theirs, grad_m, coeff = call(
        width_kernel,
        [shape((2 * rank, depth // 2))] * 2 + [shape((2, columns))] * 2,
        [SMEM] + [VMEM] * 8,
        flops=2**30,
        size=8 * 2**20,
        scratch=[pltpu.VMEM((2 * rank, depth), F32)],
    )(place, got, norm, magnitude, g_own, g_other, base, bt, a)
    a_rows = call(
        rows_kernel,
        shape((rows, columns)),
        [SMEM] + [VMEM] * 2,
        flops=2**22,
        size=2**20,
    )(place, got, coeff)

    theirs = lax.ppermute(theirs, "core", swap)
    dims = (zs, 2 * rank // zs, depth // 2 + 128)
    chunks = call(sum_kernel, shape(dims, BF16), [VMEM] * 2, size=2**20)(mine, theirs)
    got = lax.all_to_all(chunks, "z", 0, 0)

    def across(value, flip):
        return lax.ppermute(value, ("y", "x"), [(i, i ^ flip) for i in range(shards)])

    piece = call(piece_kernel, shape((3 * rows, columns)), [VMEM] * 3, size=2**18)(
        got, a_rows, across(a_rows, 2)
    )
    theirs = lax.ppermute(piece, "dp", swap)
    chunks, near = call(
        spread_kernel, [shape(dims, BF16), shape((4 * rows, columns))], [VMEM] * 2, size=2**18
    )(piece, theirs)
    full = lax.all_to_all(chunks, "z", 0, 0)
    full, *near = lax.optimization_barrier((full, near, across(near, 4), across(near, 1), across(near, 5)))
    other = lax.ppermute(full, "core", swap)
    grad_a, grad_b = call(
        last_kernel,
        [shape((2 * rank, columns)), shape((2 * rank, depth))],
        [SMEM] + [VMEM] * 6,
        size=2**21,
    )(place, full, other, *near)
    grad_b = jnp.swapaxes(grad_b.reshape(2, rank, depth), 1, 2)
    return grad_a.reshape(2, rank, columns), grad_b, grad_m


def solution(mesh):
    sizes = mesh.shape
    fine = Mesh(
        mesh.devices.reshape(sizes["dp"], sizes["fsdp"] // 2, 2, 2, sizes["tensor"] // 2),
        ("dp", "z", "core", "y", "x"),
    )
    fsdp, tensor = ("z", "core"), ("y", "x")
    return jax.shard_map(
        per_device,
        mesh=fine,
        in_specs=(
            P(("dp",) + fsdp, tensor),
            P(None, tensor, fsdp),
            P(None, tensor, None),
            P(None, None, fsdp),
            P(None, fsdp),
            P(("dp",) + tensor, fsdp),
        ),
        out_specs=(P(None, None, fsdp), P(None, tensor, None), P(None, fsdp)),
        check_vma=False,
    )
```

```python
import functools
import math

import jax
import jax.numpy as jnp
from jax import lax
from jax.experimental import pallas as pl
from jax.experimental.pallas import tpu as pltpu
from jax.sharding import Mesh, PartitionSpec as P

F32 = jnp.float32
BF16 = jnp.bfloat16
WIDTH = ("x", "y")
GROUP = ("x", "y", "dp")
VMEM = pl.BlockSpec(memory_space=pltpu.VMEM)
SMEM = pl.BlockSpec(memory_space=pltpu.SMEM)
STEP = 512

BEND = 4096.0
POWER = 250.0 / math.log2(1.0 + BEND)
SHIFT = 125.0 * math.log(2.0)


def encode(x, peak):
    size = jnp.exp(POWER * jnp.log(1.0 + jnp.abs(x) * (BEND / peak)) - SHIFT)
    return jnp.where(x < 0, -size, size)


def decode(code, peak):
    code = code.astype(F32)
    size = (jnp.exp((jnp.log(jnp.abs(code)) + SHIFT) * (1.0 / POWER)) - 1.0) * (peak / BEND)
    return jnp.where(code < 0, -size, size)


def peak_of(x):
    peak = jnp.max(jnp.max(jnp.abs(x), axis=1, keepdims=True), axis=0, keepdims=True)
    return (jnp.maximum(peak, 1e-20) * 1.01).astype(BF16).astype(F32)


def split(x):
    hi = x.astype(BF16)
    return hi, (x - hi.astype(F32)).astype(BF16)


def member_of(owner):
    y, x = divmod(owner, 4)
    return x * 2 + y


def dot(x, y, dims=((1,), (0,))):
    return lax.dot_general(x, y, (dims, ((), ())), preferred_element_type=F32)


NT = ((1,), (1,))
TN = ((0,), (0,))


def coded(value, put):
    peak = peak_of(value)
    code = encode(value, peak).astype(BF16)
    for i in range(value.shape[1] // 128):
        put(i, code[:, 128 * i : 128 * (i + 1)])
    return peak


def own_work(own_ref, base_ref, bt_ref, a_ref, part_ref, cross_ref, info_ref):
    depth, columns = base_ref.shape[1:]
    rank = a_ref.shape[1]
    tiles = columns // 128
    shards = part_ref.shape[0]
    half = own_ref.shape[0] // shards

    def put_at(first):
        def put(i, code):
            at = (first + i) * half
            for owner in range(shards):
                part_ref[member_of(owner), at : at + half, :] = code[half * owner : half * (owner + 1)]

        return put

    line = lax.broadcasted_iota(jnp.int32, (8, 128), 0)
    bt = bt_ref[...].reshape(2 * rank, depth)
    peak = coded(dot(own_ref[...], bt, NT), put_at(2 * tiles))
    peaks = jnp.where(line == 2, peak, jnp.zeros((8, 128), F32))
    for k in range(2):
        sq = jnp.zeros((8, columns), F32)
        cross = jnp.zeros((rank, columns), F32)
        for at in range(0, depth, STEP):
            rows = slice(at, at + STEP)
            bt = bt_ref[k, :, rows]
            combined = base_ref[k, rows, :].astype(F32) + dot(bt, a_ref[k], TN)
            sq += jnp.sum((combined * combined).reshape(STEP // 8, 8, columns), axis=0)
            hi, lo = split(combined)
            cross += dot(bt, hi) + dot(bt, lo)
        cross_ref[k * rank : (k + 1) * rank, :] = cross
        sq = jnp.sum(sq, axis=0, keepdims=True)
        for piece in range(2):
            part = sq.astype(BF16).astype(F32)
            sq = sq - part
            for i in range(tiles):
                row = 2 * tiles * piece + tiles * k + i
                info_ref[row : row + 1, :] = part[:, 128 * i : 128 * (i + 1)]
        peak = coded(dot(own_ref[...], base_ref[k]), put_at(tiles * k))
        peaks = jnp.where(line == k, peak, peaks)
    info_ref[4 * tiles :, :] = peaks


def early_kernel(place_ref, *refs):
    @pl.when(place_ref[1] == 1)
    def _():
        own_work(*refs)


def late_kernel(place_ref, *refs):
    @pl.when(place_ref[1] == 0)
    def _():
        own_work(*refs)


def forward_kernel(
    place_ref, early_part, early_cross, early_info, late_part, late_cross, late_info, other_ref,
    base_ref, bt_ref, out_ref, cross_ref, info_ref,
):
    shards = out_ref.shape[0]
    columns = base_ref.shape[2]
    half = other_ref.shape[0] // shards
    owned = 2 * half
    tiles = columns // 128
    info_rows = info_ref.shape[0]

    def take(part_ref, cross_in, info_in):
        for i in range(2 * tiles + 1):
            out_ref[:, owned * i : owned * i + half, :] = part_ref[:, half * i : half * (i + 1), :]
        cross_ref[...] = cross_in[...]
        info_ref[...] = info_in[...]

    @pl.when(place_ref[1] == 1)
    def _():
        take(early_part, early_cross, early_info)

    @pl.when(place_ref[1] == 0)
    def _():
        take(late_part, late_cross, late_info)

    def put_at(first):
        def put(i, code):
            at = (first + i) * owned + half
            for owner in range(shards):
                out_ref[member_of(owner), at : at + half, :] = code[half * owner : half * (owner + 1)]

        return put

    line = lax.broadcasted_iota(jnp.int32, (info_rows, 128), 0)
    info = info_ref[...]
    peak = coded(dot(other_ref[...], bt_ref[...], NT), put_at(2 * tiles))
    info = jnp.where(line == info_rows - 3, peak, info)
    for k in range(2):
        peak = coded(dot(other_ref[...], base_ref[k]), put_at(tiles * k))
        info = jnp.where(line == info_rows - 5 + k, peak, info)
    rest = info.astype(BF16)
    out_ref[:, (2 * tiles + 1) * owned :, :] = jnp.broadcast_to(rest[None], (shards,) + rest.shape)


def local_kernel(place_ref, got_ref, cot_ref, a_ref, mag_ref, cross_ref, out_ref, norm_ref):
    dp, core = place_ref[0], place_ref[1]
    shards = got_ref.shape[0]
    rank, columns = a_ref.shape[1:]
    owned = cot_ref.shape[0]
    tiles = columns // 128
    half = owned // 2
    at_extra = (2 * tiles + 1) * owned

    rests = [got_ref[source, at_extra:, :].astype(F32) for source in range(shards)]
    totals = []
    for k in range(3):
        sides = []
        for side in range(2):
            row = 4 * tiles + 3 * side + k
            parts = []
            for i in range(tiles if k < 2 else 1):
                at = (tiles * k + i) * owned + side * half
                total = None
                for source in range(shards):
                    value = decode(
                        got_ref[source, at : at + half, :], rests[source][row : row + 1, 0:1]
                    )
                    total = value if total is None else total + value
                parts.append(total)
            sides.append(jnp.concatenate(parts, axis=1) if k < 2 else parts[0])
        totals.append(jnp.concatenate(sides, axis=0))
    extra = rests[0]
    for source in range(1, shards):
        extra = extra + rests[source]
    pieces = extra[2 * tiles : 4 * tiles] + extra[: 2 * tiles]

    low = totals[2]
    low_hi, low_lo = split(low)
    outs, pres, scales = [], [], []
    for k in range(2):
        sq = jnp.concatenate(
            [pieces[tiles * k + i : tiles * k + i + 1] for i in range(tiles)], axis=1
        )
        norm = jnp.sqrt(sq + 1e-06)
        norm_ref[k : k + 1, :] = norm
        mine = slice(k * rank, (k + 1) * rank)
        pre = totals[k] + (dot(low_hi[:, mine], a_ref[k]) + dot(low_lo[:, mine], a_ref[k]))
        scale = mag_ref[k : k + 1, :] / norm
        pres.append(pre)
        scales.append(scale)
        outs.append(pre * scale)
    gate, up = outs
    quarter = half // 2
    cot = jnp.concatenate(
        [
            cot_ref[pl.ds(pl.multiple_of(start + side * quarter, quarter), quarter), :]
            for side in (core, 1 - core)
            for start in (0, half)
        ],
        axis=0,
    ).astype(F32)
    sig = 1.0 / (1.0 + jnp.exp(-gate))
    douts = (cot * up * sig * (1.0 + gate * (1.0 - sig)), cot * gate * sig)
    members = out_ref.shape[0]
    rows = 2 * rank // members
    codes, peaks, back_codes, back_peaks, ms = [], [], [], [], []
    for k in range(2):
        mine = slice(k * rank, (k + 1) * rank)
        ms.append(jnp.sum(douts[k] * pres[k], axis=0, keepdims=True))
        hi, lo = split(douts[k] * scales[k])
        grad_a = (
            dot(low_hi[:, mine], hi, TN) + dot(low_hi[:, mine], lo, TN) + dot(low_lo[:, mine], hi, TN)
        )
        back = dot(hi, a_ref[k], NT) + dot(lo, a_ref[k], NT)
        width = columns // 2
        cross = cross_ref[mine, pl.ds(pl.multiple_of(dp * width, width), width)]
        peaks.append((peak_of(grad_a), peak_of(cross)))
        codes.append((encode(grad_a, peaks[k][0]), encode(cross, peaks[k][1])))
        back_peaks.append(peak_of(back))
        back_codes.append(encode(back, back_peaks[k]))
    m_peaks = [peak_of(m) for m in ms]
    m_codes = [
        encode(m, peak)[:, 128 * i : 128 * (i + 1)]
        for m, peak in zip(ms, m_peaks)
        for i in range(tiles)
    ]
    first_half = lax.broadcasted_iota(jnp.int32, (1, 128), 1) < 64
    pair = lambda x, y: jnp.where(first_half, x, y)
    ends = [pair(*back_peaks), pair(*m_peaks), jnp.zeros((1, 128), F32)]
    spare = m_codes[rows:]
    at_back = rows * (tiles + tiles // 2 + 1)
    for j in range(members):
        k, at = divmod(j * rows, rank)
        blocks = [
            code[at : at + rows, 128 * i : 128 * (i + 1)]
            for code in codes[k]
            for i in range(code.shape[1] // 128)
        ]
        blocks.append(jnp.concatenate(spare + [pair(*peaks[k])] + ends, axis=0))
        for i in range(0, len(blocks), 2):
            two = jnp.concatenate(blocks[i : i + 2], axis=0).astype(BF16)
            out_ref[j, rows * i : rows * (i + 2), :] = two
    rest = jnp.concatenate([jnp.concatenate(back_codes, axis=1)] + m_codes[:rows], axis=0).astype(BF16)
    out_ref[:, at_back:, :] = jnp.broadcast_to(rest[None], (members,) + rest.shape)


def rows_kernel(place_ref, got_ref, coeff_ref, rows_ref):
    members = got_ref.shape[0]
    rows, columns = rows_ref.shape
    tiles = columns // 128
    height = rows * (tiles + tiles // 2 + 1)
    coeff = jnp.where(place_ref[2] < 2, coeff_ref[0:1, :], coeff_ref[1:2, :])
    tokens = [jnp.zeros((rows, 128), F32)] * tiles
    crosses = [jnp.zeros((rows, 128), F32)] * tiles
    for j in range(members):
        blocks = got_ref[j, :height, :].astype(F32)
        peaks = blocks[height - 4 : height - 3]
        token = decode(blocks[: rows * tiles], peaks[:, 0:1])
        cross = decode(blocks[rows * tiles : height - rows], peaks[:, 64:65])
        for i in range(tiles):
            tokens[i] = tokens[i] + token[rows * i : rows * (i + 1)]
        first = j % 2 * (tiles // 2)
        for i in range(tiles // 2):
            crosses[first + i] = crosses[first + i] + cross[rows * i : rows * (i + 1)]
    for i in range(tiles):
        lanes = slice(128 * i, 128 * (i + 1))
        rows_ref[:, lanes] = tokens[i] + crosses[i] * coeff[:, lanes]


def width_kernel(
    place_ref, got_ref, norm_ref, mag_ref, own_ref, other_ref, base_ref, bt_ref, a_ref,
    mine_ref, theirs_ref, grad_m_ref, coeff_ref, sum_ref,
):
    dp, core = place_ref[0], place_ref[1]
    members = got_ref.shape[0]
    shards = members // 2
    rank, columns = a_ref.shape[1:]
    tiles = columns // 128
    owned = 2 * own_ref.shape[0] // shards
    half = owned // 2
    height = got_ref.shape[1]
    at_back = height - 8 - owned
    line = lax.broadcasted_iota(jnp.int32, (2 * tiles, 1), 0)
    m = None
    for j in range(members):
        ends = got_ref[j, at_back - 16 : at_back, :].astype(F32)[8:]
        code = jnp.concatenate([got_ref[j, height - 8 :, :].astype(F32), ends[:4]], axis=0)
        part = decode(code, jnp.where(line < tiles, ends[6:7, 0:1], ends[6:7, 64:65]))
        m = part if m is None else m + part
    for k in range(2):
        norm = norm_ref[k : k + 1, :]
        m_row = jnp.concatenate([m[tiles * k + i : tiles * k + i + 1] for i in range(tiles)], axis=1)
        grad_m = m_row / norm
        grad_m_ref[k : k + 1, :] = grad_m
        coeff_ref[k : k + 1, :] = -grad_m * mag_ref[k : k + 1, :] / (norm * norm)
    backs = []
    lane = lax.broadcasted_iota(jnp.int32, (1, 2 * rank), 1)
    for j in range(shards):
        source = member_of(j) * 2 + dp
        ends = got_ref[source, at_back - 16 : at_back, :].astype(F32)
        peak = jnp.where(lane < rank, ends[13:14, 0:1], ends[13:14, 64:65])
        backs.append(decode(got_ref[source, at_back : at_back + owned, :], peak))
    total = None
    for side, ref in enumerate((own_ref, other_ref)):
        back = jnp.concatenate([b[side * half : (side + 1) * half] for b in backs], axis=0)
        hi, lo = split(back)
        both = dot(jnp.concatenate([hi, lo], axis=1), ref[...], TN)
        part = both[: 2 * rank] + both[2 * rank :]
        total = part if total is None else total + part
    sum_ref[...] = total
    a = a_ref[dp]
    hi, lo = split(a.astype(F32) * coeff_ref[pl.ds(dp, 1), :])
    weighted = jnp.concatenate([hi, lo], axis=0)
    both = dot(weighted, base_ref[dp], NT)
    small = dot(weighted, a, NT)
    small_hi, small_lo = split(small[:rank] + small[rank:])
    value = (both[:rank] + both[rank:]) + (dot(small_hi, bt_ref[dp]) + dot(small_lo, bt_ref[dp]))
    mine = pl.ds(pl.multiple_of(dp * rank, rank), rank)
    sum_ref[mine, :] += value
    width = mine_ref.shape[1]
    mine_ref[...] = sum_ref[:, pl.ds(pl.multiple_of(core * width, width), width)]
    theirs_ref[...] = sum_ref[:, pl.ds(pl.multiple_of((1 - core) * width, width), width)]


def sum_kernel(mine_ref, theirs_ref, out_ref):
    zs, rows, lanes = out_ref.shape
    part = mine_ref[...] + theirs_ref[...]
    peak = peak_of(part)
    out_ref[:, :, : lanes - 128] = encode(part, peak).reshape(zs, rows, lanes - 128).astype(BF16)
    out_ref[:, :, lanes - 128 :] = jnp.broadcast_to(peak, (zs, rows, 128)).astype(BF16)


def decoded(got_ref):
    lanes = got_ref.shape[2] - 128
    peaks = got_ref[:, :, lanes:].astype(F32)
    return decode(got_ref[:, :, :lanes], peaks[:, 0:1, 0:1])


def piece_kernel(got_ref, rows_ref, far_ref, out_ref):
    rows, width = got_ref.shape[1], got_ref.shape[2] - 128
    columns = out_ref.shape[1]
    out_ref[:rows, :width] = jnp.sum(decoded(got_ref), axis=0)
    out_ref[:rows, width:] = jnp.zeros((rows, columns - width), F32)
    out_ref[rows : 2 * rows, :] = rows_ref[...]
    out_ref[2 * rows :, :] = far_ref[...]


def spread_kernel(mine_ref, theirs_ref, out_ref, rows_ref):
    zs, rows, lanes = out_ref.shape
    width = lanes - 128
    piece = mine_ref[:rows, :width] + theirs_ref[:rows, :width]
    peak = peak_of(piece)
    code = jnp.concatenate([encode(piece, peak), jnp.broadcast_to(peak, (rows, 128))], axis=1)
    out_ref[...] = jnp.broadcast_to(code[None], (zs, rows, lanes)).astype(BF16)
    rows_ref[: 2 * rows, :] = mine_ref[rows:, :]
    rows_ref[2 * rows :, :] = theirs_ref[rows:, :]


def last_kernel(place_ref, own_ref, other_ref, r0_ref, r1_ref, r2_ref, r3_ref, grad_a_ref, grad_b_ref):
    core, member = place_ref[1], place_ref[3]
    count = own_ref.shape[1]
    for near, ref in enumerate((r0_ref, r1_ref, r2_ref, r3_ref)):
        for i, far in enumerate((0, 8, 1, 9)):
            at = pl.multiple_of(jnp.bitwise_xor(member, 2 * near + far) * count, count)
            grad_a_ref[pl.ds(at, count), :] = ref[count * i : count * (i + 1), :]
    rows, columns = grad_b_ref.shape
    width = columns // 2
    for side, ref in ((core, own_ref), (1 - core, other_ref)):
        lanes = pl.ds(pl.multiple_of(side * width, width), width)
        grad_b_ref[:, lanes] = decoded(ref).reshape(rows, width)


def call(kernel, outs, in_specs, flops=0, size=0, scratch=()):
    return pl.pallas_call(
        kernel,
        out_shape=outs,
        in_specs=in_specs,
        out_specs=[VMEM] * len(outs) if isinstance(outs, (list, tuple)) else VMEM,
        scratch_shapes=scratch,
        compiler_params=pltpu.CompilerParams(vmem_limit_bytes=24 * 2**20),
        cost_estimate=pl.CostEstimate(flops=flops, bytes_accessed=size, transcendentals=0),
    )


def shape(dims, dtype=F32):
    return jax.ShapeDtypeStruct(dims, dtype)


def per_device(tokens, base, b, a, magnitude, cotangent):
    dp = lax.axis_index("dp")
    core = lax.axis_index("core")
    depth, columns = base.shape[1:]
    rank = a.shape[1]
    shards = lax.axis_size(WIDTH)
    members = 2 * shards
    zs = lax.axis_size("z")
    own = 2 * zs * tokens.shape[0] // shards
    rows = 2 * rank // members
    tiles = columns // 128
    swap = [(0, 1), (1, 0)]
    bt = jnp.swapaxes(b, 1, 2)
    place = jnp.stack([dp, core, lax.axis_index("x"), lax.axis_index(GROUP)]).astype(jnp.int32)

    g_own = lax.all_gather(tokens, "z", axis=0, tiled=True)
    g_own, place = lax.optimization_barrier((g_own, place))
    info_rows = 4 * tiles + 8
    outs = [
        shape((shards, (2 * tiles + 1) * own // 2, 128), BF16),
        shape((2 * rank, columns)),
        shape((info_rows, 128)),
    ]
    early, late = (
        functools.partial(
            call,
            kernel,
            outs,
            [SMEM] + [VMEM] * 4,
            flops=2**30,
            size=4 * 2**20,
        )()
        for kernel in (early_kernel, late_kernel)
    )
    first = early(place, g_own, base, bt, a)
    g_own, first = lax.optimization_barrier((g_own, first))
    g_other = lax.ppermute(g_own, "core", swap)
    second = late(place, g_own, base, bt, a)
    payload, cross = call(
        forward_kernel,
        [shape((shards, (2 * tiles + 1) * own + info_rows, 128), BF16), outs[1]],
        [SMEM] + [VMEM] * 9,
        flops=2**30,
        size=8 * 2**20,
        scratch=[pltpu.VMEM((info_rows, 128), F32)],
    )(place, *first, *second, g_other, base, bt.reshape(2 * rank, depth))
    got = lax.all_to_all(payload, WIDTH, 0, 0)

    height = rows * (tiles + tiles // 2 + 1) + own + 8
    sends, norm = call(
        local_kernel,
        [shape((members, height, 128), BF16), shape((2, columns))],
        [SMEM] + [VMEM] * 5,
        flops=2**27,
        size=4 * 2**20,
    )(place, got, cotangent, a, magnitude, cross)
    got = lax.all_to_all(sends, GROUP, 0, 0)

    mine, theirs, grad_m, coeff = call(
        width_kernel,
        [shape((2 * rank, depth // 2))] * 2 + [shape((2, columns))] * 2,
        [SMEM] + [VMEM] * 8,
        flops=2**30,
        size=8 * 2**20,
        scratch=[pltpu.VMEM((2 * rank, depth), F32)],
    )(place, got, norm, magnitude, g_own, g_other, base, bt, a)
    a_rows = call(
        rows_kernel,
        shape((rows, columns)),
        [SMEM] + [VMEM] * 2,
        flops=2**22,
        size=2**20,
    )(place, got, coeff)

    theirs = lax.ppermute(theirs, "core", swap)
    dims = (zs, 2 * rank // zs, depth // 2 + 128)
    chunks = call(sum_kernel, shape(dims, BF16), [VMEM] * 2, size=2**20)(mine, theirs)
    got = lax.all_to_all(chunks, "z", 0, 0)

    def across(value, flip):
        return lax.ppermute(value, ("y", "x"), [(i, i ^ flip) for i in range(shards)])

    piece = call(piece_kernel, shape((3 * rows, columns)), [VMEM] * 3, size=2**18)(
        got, a_rows, across(a_rows, 2)
    )
    theirs = lax.ppermute(piece, "dp", swap)
    chunks, near = call(
        spread_kernel, [shape(dims, BF16), shape((4 * rows, columns))], [VMEM] * 2, size=2**18
    )(piece, theirs)
    full = lax.all_to_all(chunks, "z", 0, 0)
    full, *near = lax.optimization_barrier((full, near, across(near, 4), across(near, 1), across(near, 5)))
    other = lax.ppermute(full, "core", swap)
    grad_a, grad_b = call(
        last_kernel,
        [shape((2 * rank, columns)), shape((2 * rank, depth))],
        [SMEM] + [VMEM] * 6,
        size=2**21,
    )(place, full, other, *near)
    grad_b = jnp.swapaxes(grad_b.reshape(2, rank, depth), 1, 2)
    return grad_a.reshape(2, rank, columns), grad_b, grad_m


def solution(mesh):
    sizes = mesh.shape
    fine = Mesh(
        mesh.devices.reshape(sizes["dp"], sizes["fsdp"] // 2, 2, 2, sizes["tensor"] // 2),
        ("dp", "z", "core", "y", "x"),
    )
    fsdp, tensor = ("z", "core"), ("y", "x")
    return jax.shard_map(
        per_device,
        mesh=fine,
        in_specs=(
            P(("dp",) + fsdp, tensor),
            P(None, tensor, fsdp),
            P(None, tensor, None),
            P(None, None, fsdp),
            P(None, fsdp),
            P(("dp",) + tensor, fsdp),
        ),
        out_specs=(P(None, None, fsdp), P(None, tensor, None), P(None, fsdp)),
        check_vma=False,
    )
```

```python
import functools
import math

import jax
import jax.numpy as jnp
from jax import lax
from jax.experimental import pallas as pl
from jax.experimental.pallas import tpu as pltpu
from jax.sharding import Mesh, PartitionSpec as P

F32 = jnp.float32
BF16 = jnp.bfloat16
WIDTH = ("x", "y")
GROUP = ("x", "y", "dp")
VMEM = pl.BlockSpec(memory_space=pltpu.VMEM)
SMEM = pl.BlockSpec(memory_space=pltpu.SMEM)
STEP = 512

BEND = 1024.0
POWER = 250.0 / math.log2(1.0 + BEND)
SHIFT = 125.0
LN2 = math.log(2.0)


def encode(x, peak):
    size = jnp.exp2(jnp.log(1.0 + jnp.abs(x) * (BEND / peak)) * (POWER / LN2) - SHIFT)
    return jnp.where(x < 0, -size, size)


def decode(code, peak):
    code = code.astype(F32)
    scale = peak / BEND
    size = jnp.exp2(jnp.log(jnp.abs(code)) * (1.0 / (POWER * LN2)) + SHIFT / POWER) * scale - scale
    return jnp.where(code < 0, -size, size)


def peak_of(x):
    peak = jnp.max(jnp.max(jnp.abs(x), axis=1, keepdims=True), axis=0, keepdims=True)
    return (jnp.maximum(peak, 1e-20) * 1.01).astype(BF16).astype(F32)


def split(x):
    hi = x.astype(BF16)
    return hi, (x - hi.astype(F32)).astype(BF16)


def member_of(owner):
    y, x = divmod(owner, 4)
    return x * 2 + y


def dot(x, y, dims=((1,), (0,))):
    return lax.dot_general(x, y, (dims, ((), ())), preferred_element_type=F32)


NT = ((1,), (1,))
TN = ((0,), (0,))


def coded(value, put):
    peak = peak_of(value)
    code = encode(value, peak).astype(BF16)
    for i in range(value.shape[1] // 128):
        put(i, code[:, 128 * i : 128 * (i + 1)])
    return peak


def own_work(own_ref, base_ref, low_ref, part_ref, cross_ref, info_ref):
    depth, columns = base_ref.shape[1:]
    rank = low_ref.shape[1]
    bt_ref, a_ref = low_ref.at[:, :, :depth], low_ref.at[:, :, depth:]
    tiles = columns // 128
    shards = part_ref.shape[0]
    half = own_ref.shape[0] // shards

    def put_at(first):
        def put(i, code):
            at = (first + i) * half
            for owner in range(shards):
                part_ref[member_of(owner), at : at + half, :] = code[half * owner : half * (owner + 1)]

        return put

    line = lax.broadcasted_iota(jnp.int32, (8, 128), 0)
    bt = bt_ref[...].reshape(2 * rank, depth)
    peak = coded(dot(own_ref[...], bt, NT), put_at(2 * tiles))
    peaks = jnp.where(line == 2, peak, jnp.zeros((8, 128), F32))
    for k in range(2):
        sq = jnp.zeros((8, columns), F32)
        for at in range(0, depth, STEP):
            rows = slice(at, at + STEP)
            combined = base_ref[k, rows, :].astype(F32) + dot(bt_ref[k, :, rows], a_ref[k], TN)
            sq += jnp.sum((combined * combined).reshape(STEP // 8, 8, columns), axis=0)
        bt = bt_ref[k]
        square = dot(bt, bt, NT)
        hi, lo = split(square)
        rest = (square - hi.astype(F32) - lo.astype(F32)).astype(BF16)
        cross_ref[k * rank : (k + 1) * rank, :] = dot(bt, base_ref[k]) + (
            dot(hi, a_ref[k]) + (dot(lo, a_ref[k]) + dot(rest, a_ref[k]))
        )
        sq = jnp.sum(sq, axis=0, keepdims=True)
        for piece in range(2):
            part = sq.astype(BF16).astype(F32)
            sq = sq - part
            for i in range(tiles):
                row = 2 * tiles * piece + tiles * k + i
                info_ref[row : row + 1, :] = part[:, 128 * i : 128 * (i + 1)]
        peak = coded(dot(own_ref[...], base_ref[k]), put_at(tiles * k))
        peaks = jnp.where(line == k, peak, peaks)
    info_ref[4 * tiles :, :] = peaks


def early_kernel(place_ref, *refs):
    @pl.when(place_ref[1] == 1)
    def _():
        own_work(*refs)


def late_kernel(place_ref, *refs):
    @pl.when(place_ref[1] == 0)
    def _():
        own_work(*refs)


def forward_kernel(
    place_ref, early_part, early_info, late_part, late_info, other_ref, base_ref, low_ref, out_ref, info_ref
):
    shards = out_ref.shape[0]
    depth, columns = base_ref.shape[1:]
    bt = low_ref[:, :, :depth].reshape(2 * low_ref.shape[1], depth)
    half = other_ref.shape[0] // shards
    owned = 2 * half
    tiles = columns // 128
    info_rows = info_ref.shape[0]

    def take(part_ref, info_in):
        for i in range(2 * tiles + 1):
            out_ref[:, owned * i : owned * i + half, :] = part_ref[:, half * i : half * (i + 1), :]
        info_ref[...] = info_in[...]

    @pl.when(place_ref[1] == 1)
    def _():
        take(early_part, early_info)

    @pl.when(place_ref[1] == 0)
    def _():
        take(late_part, late_info)

    def put_at(first):
        def put(i, code):
            at = (first + i) * owned + half
            for owner in range(shards):
                out_ref[member_of(owner), at : at + half, :] = code[half * owner : half * (owner + 1)]

        return put

    line = lax.broadcasted_iota(jnp.int32, (info_rows, 128), 0)
    info = info_ref[...]
    peak = coded(dot(other_ref[...], bt, NT), put_at(2 * tiles))
    info = jnp.where(line == info_rows - 3, peak, info)
    for k in range(2):
        peak = coded(dot(other_ref[...], base_ref[k]), put_at(tiles * k))
        info = jnp.where(line == info_rows - 5 + k, peak, info)
    rest = info.astype(BF16)
    out_ref[:, (2 * tiles + 1) * owned :, :] = jnp.broadcast_to(rest[None], (shards,) + rest.shape)


def local_kernel(
    place_ref, got_ref, cot_ref, low_ref, mag_ref, early_cross, late_cross, out_ref, norm_ref
):
    dp, core = place_ref[0], place_ref[1]
    shards = got_ref.shape[0]
    columns = cot_ref.shape[1]
    rank = low_ref.shape[1]
    a_ref = low_ref.at[:, :, low_ref.shape[2] - columns :]
    owned = cot_ref.shape[0]
    tiles = columns // 128
    half = owned // 2
    at_extra = (2 * tiles + 1) * owned

    rests = [got_ref[source, at_extra:, :].astype(F32) for source in range(shards)]
    totals = []
    for k in range(3):
        sides = []
        for side in range(2):
            row = 4 * tiles + 3 * side + k
            parts = []
            for i in range(tiles if k < 2 else 1):
                at = (tiles * k + i) * owned + side * half
                total = None
                for source in range(shards):
                    value = decode(
                        got_ref[source, at : at + half, :], rests[source][row : row + 1, 0:1]
                    )
                    total = value if total is None else total + value
                parts.append(total)
            sides.append(jnp.concatenate(parts, axis=1) if k < 2 else parts[0])
        totals.append(jnp.concatenate(sides, axis=0))
    extra = rests[0]
    for source in range(1, shards):
        extra = extra + rests[source]
    pieces = extra[2 * tiles : 4 * tiles] + extra[: 2 * tiles]

    low = totals[2]
    low_hi, low_lo = split(low)
    outs, pres, scales = [], [], []
    for k in range(2):
        sq = jnp.concatenate(
            [pieces[tiles * k + i : tiles * k + i + 1] for i in range(tiles)], axis=1
        )
        norm = jnp.sqrt(sq + 1e-06)
        norm_ref[k : k + 1, :] = norm
        mine = slice(k * rank, (k + 1) * rank)
        pre = totals[k] + (dot(low_hi[:, mine], a_ref[k]) + dot(low_lo[:, mine], a_ref[k]))
        scale = mag_ref[k : k + 1, :] / norm
        pres.append(pre)
        scales.append(scale)
        outs.append(pre * scale)
    gate, up = outs
    quarter = half // 2
    cot = jnp.concatenate(
        [
            cot_ref[pl.ds(pl.multiple_of(start + side * quarter, quarter), quarter), :]
            for side in (core, 1 - core)
            for start in (0, half)
        ],
        axis=0,
    ).astype(F32)
    sig = 1.0 / (1.0 + jnp.exp(-gate))
    douts = (cot * up * sig * (1.0 + gate * (1.0 - sig)), cot * gate * sig)
    members = out_ref.shape[0]
    rows = 2 * rank // members
    codes, peaks, back_codes, back_peaks, ms = [], [], [], [], []
    for k in range(2):
        mine = slice(k * rank, (k + 1) * rank)
        ms.append(jnp.sum(douts[k] * pres[k], axis=0, keepdims=True))
        hi, lo = split(douts[k] * scales[k])
        grad_a = (
            dot(low_hi[:, mine], hi, TN) + dot(low_hi[:, mine], lo, TN) + dot(low_lo[:, mine], hi, TN)
        )
        back = dot(hi, a_ref[k], NT) + dot(lo, a_ref[k], NT)
        width = columns // 2
        lanes = pl.ds(pl.multiple_of(dp * width, width), width)
        cross = jnp.where(core == 1, early_cross[mine, lanes], late_cross[mine, lanes])
        peaks.append((peak_of(grad_a), peak_of(cross)))
        codes.append((encode(grad_a, peaks[k][0]), encode(cross, peaks[k][1])))
        back_peaks.append(peak_of(back))
        back_codes.append(encode(back, back_peaks[k]))
    m_peaks = [peak_of(m) for m in ms]
    m_codes = [
        encode(m, peak)[:, 128 * i : 128 * (i + 1)]
        for m, peak in zip(ms, m_peaks)
        for i in range(tiles)
    ]
    first_half = lax.broadcasted_iota(jnp.int32, (1, 128), 1) < 64
    pair = lambda x, y: jnp.where(first_half, x, y)
    ends = [pair(*back_peaks), pair(*m_peaks), jnp.zeros((1, 128), F32)]
    spare = m_codes[rows:]
    at_back = rows * (tiles + tiles // 2 + 1)
    for j in range(members):
        k, at = divmod(j * rows, rank)
        blocks = [
            code[at : at + rows, 128 * i : 128 * (i + 1)]
            for code in codes[k]
            for i in range(code.shape[1] // 128)
        ]
        blocks.append(jnp.concatenate(spare + [pair(*peaks[k])] + ends, axis=0))
        for i in range(0, len(blocks), 2):
            two = jnp.concatenate(blocks[i : i + 2], axis=0).astype(BF16)
            out_ref[j, rows * i : rows * (i + 2), :] = two
    rest = jnp.concatenate([jnp.concatenate(back_codes, axis=1)] + m_codes[:rows], axis=0).astype(BF16)
    out_ref[:, at_back:, :] = jnp.broadcast_to(rest[None], (members,) + rest.shape)


def rows_kernel(place_ref, got_ref, coeff_ref, rows_ref):
    members = got_ref.shape[0]
    rows, columns = rows_ref.shape
    tiles = columns // 128
    height = rows * (tiles + tiles // 2 + 1)
    coeff = jnp.where(place_ref[2] < 2, coeff_ref[0:1, :], coeff_ref[1:2, :])
    tokens = [jnp.zeros((rows, 128), F32)] * tiles
    crosses = [jnp.zeros((rows, 128), F32)] * tiles
    for j in range(members):
        blocks = got_ref[j, :height, :].astype(F32)
        peaks = blocks[height - 4 : height - 3]
        token = decode(blocks[: rows * tiles], peaks[:, 0:1])
        cross = decode(blocks[rows * tiles : height - rows], peaks[:, 64:65])
        for i in range(tiles):
            tokens[i] = tokens[i] + token[rows * i : rows * (i + 1)]
        first = j % 2 * (tiles // 2)
        for i in range(tiles // 2):
            crosses[first + i] = crosses[first + i] + cross[rows * i : rows * (i + 1)]
    for i in range(tiles):
        lanes = slice(128 * i, 128 * (i + 1))
        rows_ref[:, lanes] = tokens[i] + crosses[i] * coeff[:, lanes]


def width_kernel(
    place_ref, got_ref, norm_ref, mag_ref, own_ref, other_ref, base_ref, low_ref,
    mine_ref, theirs_ref, grad_m_ref, coeff_ref, sum_ref,
):
    dp, core = place_ref[0], place_ref[1]
    members = got_ref.shape[0]
    shards = members // 2
    depth, columns = base_ref.shape[1:]
    rank = low_ref.shape[1]
    tiles = columns // 128
    owned = 2 * own_ref.shape[0] // shards
    half = owned // 2
    height = got_ref.shape[1]
    at_back = height - 8 - owned
    line = lax.broadcasted_iota(jnp.int32, (2 * tiles, 1), 0)
    m = None
    for j in range(members):
        ends = got_ref[j, at_back - 16 : at_back, :].astype(F32)[8:]
        code = jnp.concatenate([got_ref[j, height - 8 :, :].astype(F32), ends[:4]], axis=0)
        part = decode(code, jnp.where(line < tiles, ends[6:7, 0:1], ends[6:7, 64:65]))
        m = part if m is None else m + part
    for k in range(2):
        norm = norm_ref[k : k + 1, :]
        m_row = jnp.concatenate([m[tiles * k + i : tiles * k + i + 1] for i in range(tiles)], axis=1)
        grad_m = m_row / norm
        grad_m_ref[k : k + 1, :] = grad_m
        coeff_ref[k : k + 1, :] = -grad_m * mag_ref[k : k + 1, :] / (norm * norm)
    backs = []
    lane = lax.broadcasted_iota(jnp.int32, (1, 2 * rank), 1)
    for j in range(shards):
        source = member_of(j) * 2 + dp
        ends = got_ref[source, at_back - 16 : at_back, :].astype(F32)
        peak = jnp.where(lane < rank, ends[13:14, 0:1], ends[13:14, 64:65])
        backs.append(decode(got_ref[source, at_back : at_back + owned, :], peak))
    total = None
    for side, ref in enumerate((own_ref, other_ref)):
        back = jnp.concatenate([b[side * half : (side + 1) * half] for b in backs], axis=0)
        hi, lo = split(back)
        both = dot(jnp.concatenate([hi, lo], axis=1), ref[...], TN)
        part = both[: 2 * rank] + both[2 * rank :]
        total = part if total is None else total + part
    sum_ref[...] = total
    a = low_ref[dp, :, depth:]
    bt = low_ref[dp, :, :depth]
    hi, lo = split(a.astype(F32) * coeff_ref[pl.ds(dp, 1), :])
    weighted = jnp.concatenate([hi, lo], axis=0)
    both = dot(weighted, base_ref[dp], NT)
    small = dot(weighted, a, NT)
    small_hi, small_lo = split(small[:rank] + small[rank:])
    value = (both[:rank] + both[rank:]) + (dot(small_hi, bt) + dot(small_lo, bt))
    mine = pl.ds(pl.multiple_of(dp * rank, rank), rank)
    sum_ref[mine, :] += value
    width = mine_ref.shape[1]
    mine_ref[...] = sum_ref[:, pl.ds(pl.multiple_of(core * width, width), width)]
    theirs_ref[...] = sum_ref[:, pl.ds(pl.multiple_of((1 - core) * width, width), width)]


def sum_kernel(mine_ref, theirs_ref, out_ref):
    zs, rows, lanes = out_ref.shape
    part = mine_ref[...] + theirs_ref[...]
    peak = peak_of(part)
    out_ref[:, :, : lanes - 128] = encode(part, peak).reshape(zs, rows, lanes - 128).astype(BF16)
    out_ref[:, :, lanes - 128 :] = jnp.broadcast_to(peak, (zs, rows, 128)).astype(BF16)


def decoded(got_ref):
    lanes = got_ref.shape[2] - 128
    peaks = got_ref[:, :, lanes:].astype(F32)
    return decode(got_ref[:, :, :lanes], peaks[:, 0:1, 0:1])


def piece_kernel(got_ref, rows_ref, far_ref, out_ref):
    rows, width = got_ref.shape[1], got_ref.shape[2] - 128
    columns = out_ref.shape[1]
    out_ref[:rows, :width] = jnp.sum(decoded(got_ref), axis=0)
    out_ref[:rows, width:] = jnp.zeros((rows, columns - width), F32)
    out_ref[rows : 2 * rows, :] = rows_ref[...]
    out_ref[2 * rows :, :] = far_ref[...]


def spread_kernel(mine_ref, theirs_ref, out_ref, rows_ref):
    zs, rows, lanes = out_ref.shape
    width = lanes - 128
    piece = mine_ref[:rows, :width] + theirs_ref[:rows, :width]
    peak = peak_of(piece)
    code = jnp.concatenate([encode(piece, peak), jnp.broadcast_to(peak, (rows, 128))], axis=1)
    out_ref[...] = jnp.broadcast_to(code[None], (zs, rows, lanes)).astype(BF16)
    rows_ref[: 2 * rows, :] = mine_ref[rows:, :]
    rows_ref[2 * rows :, :] = theirs_ref[rows:, :]


def last_kernel(place_ref, own_ref, other_ref, r0_ref, r1_ref, r2_ref, r3_ref, grad_a_ref, grad_b_ref):
    core, member = place_ref[1], place_ref[3]
    count = own_ref.shape[1]
    for near, ref in enumerate((r0_ref, r1_ref, r2_ref, r3_ref)):
        for i, far in enumerate((0, 8, 1, 9)):
            at = pl.multiple_of(jnp.bitwise_xor(member, 2 * near + far) * count, count)
            grad_a_ref[pl.ds(at, count), :] = ref[count * i : count * (i + 1), :]
    rows, columns = grad_b_ref.shape
    width = columns // 2
    for side, ref in ((core, own_ref), (1 - core, other_ref)):
        lanes = pl.ds(pl.multiple_of(side * width, width), width)
        grad_b_ref[:, lanes] = decoded(ref).reshape(rows, width)


def call(kernel, outs, in_specs, flops=0, size=0, scratch=()):
    return pl.pallas_call(
        kernel,
        out_shape=outs,
        in_specs=in_specs,
        out_specs=[VMEM] * len(outs) if isinstance(outs, (list, tuple)) else VMEM,
        scratch_shapes=scratch,
        compiler_params=pltpu.CompilerParams(vmem_limit_bytes=24 * 2**20),
        cost_estimate=pl.CostEstimate(flops=flops, bytes_accessed=size, transcendentals=0),
    )


def shape(dims, dtype=F32):
    return jax.ShapeDtypeStruct(dims, dtype)


def per_device(tokens, base, b, a, magnitude, cotangent):
    dp = lax.axis_index("dp")
    core = lax.axis_index("core")
    depth, columns = base.shape[1:]
    rank = a.shape[1]
    shards = lax.axis_size(WIDTH)
    members = 2 * shards
    zs = lax.axis_size("z")
    own = 2 * zs * tokens.shape[0] // shards
    rows = 2 * rank // members
    tiles = columns // 128
    swap = [(0, 1), (1, 0)]
    low = jnp.concatenate([jnp.swapaxes(b, 1, 2), a], axis=2)
    place = jnp.stack([dp, core, lax.axis_index("x"), lax.axis_index(GROUP)]).astype(jnp.int32)

    g_own = lax.all_gather(tokens, "z", axis=0, tiled=True)
    g_own, place = lax.optimization_barrier((g_own, place))
    info_rows = 4 * tiles + 8
    outs = [
        shape((shards, (2 * tiles + 1) * own // 2, 128), BF16),
        shape((2 * rank, columns)),
        shape((info_rows, 128)),
    ]
    early, late = (
        functools.partial(
            call,
            kernel,
            outs,
            [SMEM] + [VMEM] * 3,
            flops=2**30,
            size=4 * 2**20,
        )()
        for kernel in (early_kernel, late_kernel)
    )
    first = early(place, g_own, base, low)
    g_own, first = lax.optimization_barrier((g_own, first))
    g_other = lax.ppermute(g_own, "core", swap)
    second = late(place, g_own, base, low)
    payload = call(
        forward_kernel,
        shape((shards, (2 * tiles + 1) * own + info_rows, 128), BF16),
        [SMEM] + [VMEM] * 7,
        flops=2**30,
        size=8 * 2**20,
        scratch=[pltpu.VMEM((info_rows, 128), F32)],
    )(place, first[0], first[2], second[0], second[2], g_other, base, low)
    got = lax.all_to_all(payload, WIDTH, 0, 0)

    height = rows * (tiles + tiles // 2 + 1) + own + 8
    sends, norm = call(
        local_kernel,
        [shape((members, height, 128), BF16), shape((2, columns))],
        [SMEM] + [VMEM] * 6,
        flops=2**27,
        size=4 * 2**20,
    )(place, got, cotangent, low, magnitude, first[1], second[1])
    got = lax.all_to_all(sends, GROUP, 0, 0)

    mine, theirs, grad_m, coeff = call(
        width_kernel,
        [shape((2 * rank, depth // 2))] * 2 + [shape((2, columns))] * 2,
        [SMEM] + [VMEM] * 7,
        flops=2**30,
        size=8 * 2**20,
        scratch=[pltpu.VMEM((2 * rank, depth), F32)],
    )(place, got, norm, magnitude, g_own, g_other, base, low)
    a_rows = call(
        rows_kernel,
        shape((rows, columns)),
        [SMEM] + [VMEM] * 2,
        flops=2**22,
        size=2**20,
    )(place, got, coeff)

    theirs = lax.ppermute(theirs, "core", swap)
    dims = (zs, 2 * rank // zs, depth // 2 + 128)
    chunks = call(sum_kernel, shape(dims, BF16), [VMEM] * 2, size=2**20)(mine, theirs)
    got = lax.all_to_all(chunks, "z", 0, 0)

    def across(value, flip):
        return lax.ppermute(value, ("y", "x"), [(i, i ^ flip) for i in range(shards)])

    piece = call(piece_kernel, shape((3 * rows, columns)), [VMEM] * 3, size=2**18)(
        got, a_rows, across(a_rows, 2)
    )
    theirs = lax.ppermute(piece, "dp", swap)
    chunks, near = call(
        spread_kernel, [shape(dims, BF16), shape((4 * rows, columns))], [VMEM] * 2, size=2**18
    )(piece, theirs)
    full = lax.all_to_all(chunks, "z", 0, 0)
    full, *near = lax.optimization_barrier((full, near, across(near, 4), across(near, 1), across(near, 5)))
    other = lax.ppermute(full, "core", swap)
    grad_a, grad_b = call(
        last_kernel,
        [shape((2 * rank, columns)), shape((2 * rank, depth))],
        [SMEM] + [VMEM] * 6,
        size=2**21,
    )(place, full, other, *near)
    grad_b = jnp.swapaxes(grad_b.reshape(2, rank, depth), 1, 2)
    return grad_a.reshape(2, rank, columns), grad_b, grad_m


def solution(mesh):
    sizes = mesh.shape
    fine = Mesh(
        mesh.devices.reshape(sizes["dp"], sizes["fsdp"] // 2, 2, 2, sizes["tensor"] // 2),
        ("dp", "z", "core", "y", "x"),
    )
    fsdp, tensor = ("z", "core"), ("y", "x")
    return jax.shard_map(
        per_device,
        mesh=fine,
        in_specs=(
            P(("dp",) + fsdp, tensor),
            P(None, tensor, fsdp),
            P(None, tensor, None),
            P(None, None, fsdp),
            P(None, fsdp),
            P(("dp",) + tensor, fsdp),
        ),
        out_specs=(P(None, None, fsdp), P(None, tensor, None), P(None, fsdp)),
        check_vma=False,
    )
```

```python
import functools
import math

import jax
import jax.numpy as jnp
from jax import lax
from jax.experimental import pallas as pl
from jax.experimental.pallas import tpu as pltpu
from jax.sharding import Mesh, PartitionSpec as P

F32 = jnp.float32
BF16 = jnp.bfloat16
WIDTH = ("x", "y")
GROUP = ("x", "y", "dp")
VMEM = pl.BlockSpec(memory_space=pltpu.VMEM)
SMEM = pl.BlockSpec(memory_space=pltpu.SMEM)
STEP = 512

BEND = 1024.0
POWER = 250.0 / math.log2(1.0 + BEND)
SHIFT = 125.0
LN2 = math.log(2.0)


def encode(x, peak):
    size = jnp.exp2(jnp.log(1.0 + jnp.abs(x) * (BEND / peak)) * (POWER / LN2) - SHIFT)
    return jnp.where(x < 0, -size, size)


def decode(code, peak):
    code = code.astype(F32)
    scale = peak / BEND
    size = jnp.exp2(jnp.log(jnp.abs(code)) * (1.0 / (POWER * LN2)) + SHIFT / POWER) * scale - scale
    return jnp.where(code < 0, -size, size)


def peak_of(x):
    peak = jnp.max(jnp.max(jnp.abs(x), axis=1, keepdims=True), axis=0, keepdims=True)
    return (jnp.maximum(peak, 1e-20) * 1.01).astype(BF16).astype(F32)


def split(x):
    hi = x.astype(BF16)
    return hi, (x - hi.astype(F32)).astype(BF16)


def member_of(owner):
    y, x = divmod(owner, 4)
    return x * 2 + y


def dot(x, y, dims=((1,), (0,))):
    return lax.dot_general(x, y, (dims, ((), ())), preferred_element_type=F32)


NT = ((1,), (1,))
TN = ((0,), (0,))


def coded(value, put):
    peak = peak_of(value)
    code = encode(value, peak).astype(BF16)
    for i in range(value.shape[1] // 128):
        put(i, code[:, 128 * i : 128 * (i + 1)])
    return peak


def own_work(own_ref, base_ref, low_ref, part_ref, cross_ref, info_ref):
    depth, columns = base_ref.shape[1:]
    rank = low_ref.shape[1]
    bt_ref, a_ref = low_ref.at[:, :, :depth], low_ref.at[:, :, depth:]
    tiles = columns // 128
    shards = part_ref.shape[0]
    half = own_ref.shape[0] // shards

    def put_at(first):
        def put(i, code):
            at = (first + i) * half
            for owner in range(shards):
                part_ref[member_of(owner), at : at + half, :] = code[half * owner : half * (owner + 1)]

        return put

    line = lax.broadcasted_iota(jnp.int32, (8, 128), 0)
    bt = bt_ref[...].reshape(2 * rank, depth)
    peak = coded(dot(own_ref[...], bt, NT), put_at(2 * tiles))
    peaks = jnp.where(line == 2, peak, jnp.zeros((8, 128), F32))
    for k in range(2):
        sq = jnp.zeros((8, columns), F32)
        for at in range(0, depth, STEP):
            rows = slice(at, at + STEP)
            combined = base_ref[k, rows, :].astype(F32) + dot(bt_ref[k, :, rows], a_ref[k], TN)
            sq += jnp.sum((combined * combined).reshape(STEP // 8, 8, columns), axis=0)
        bt = bt_ref[k]
        square = dot(bt, bt, NT)
        hi, lo = split(square)
        rest = (square - hi.astype(F32) - lo.astype(F32)).astype(BF16)
        cross_ref[k * rank : (k + 1) * rank, :] = dot(bt, base_ref[k]) + (
            dot(hi, a_ref[k]) + (dot(lo, a_ref[k]) + dot(rest, a_ref[k]))
        )
        sq = jnp.sum(sq, axis=0, keepdims=True)
        for piece in range(2):
            part = sq.astype(BF16).astype(F32)
            sq = sq - part
            for i in range(tiles):
                row = 2 * tiles * piece + tiles * k + i
                info_ref[row : row + 1, :] = part[:, 128 * i : 128 * (i + 1)]
        peak = coded(dot(own_ref[...], base_ref[k]), put_at(tiles * k))
        peaks = jnp.where(line == k, peak, peaks)
    info_ref[4 * tiles :, :] = peaks


def early_kernel(place_ref, *refs):
    @pl.when(place_ref[1] == 1)
    def _():
        own_work(*refs)


def late_kernel(place_ref, *refs):
    @pl.when(place_ref[1] == 0)
    def _():
        own_work(*refs)


def forward_kernel(
    place_ref, early_part, early_info, late_part, late_info, other_ref, base_ref, low_ref, out_ref, info_ref
):
    shards = out_ref.shape[0]
    depth, columns = base_ref.shape[1:]
    bt = low_ref[:, :, :depth].reshape(2 * low_ref.shape[1], depth)
    half = other_ref.shape[0] // shards
    owned = 2 * half
    tiles = columns // 128
    info_rows = info_ref.shape[0]

    def take(part_ref, info_in):
        for i in range(2 * tiles + 1):
            out_ref[:, owned * i : owned * i + half, :] = part_ref[:, half * i : half * (i + 1), :]
        info_ref[...] = info_in[...]

    @pl.when(place_ref[1] == 1)
    def _():
        take(early_part, early_info)

    @pl.when(place_ref[1] == 0)
    def _():
        take(late_part, late_info)

    def put_at(first):
        def put(i, code):
            at = (first + i) * owned + half
            for owner in range(shards):
                out_ref[member_of(owner), at : at + half, :] = code[half * owner : half * (owner + 1)]

        return put

    line = lax.broadcasted_iota(jnp.int32, (info_rows, 128), 0)
    info = info_ref[...]
    peak = coded(dot(other_ref[...], bt, NT), put_at(2 * tiles))
    info = jnp.where(line == info_rows - 3, peak, info)
    for k in range(2):
        peak = coded(dot(other_ref[...], base_ref[k]), put_at(tiles * k))
        info = jnp.where(line == info_rows - 5 + k, peak, info)
    rest = info.astype(BF16)
    out_ref[:, (2 * tiles + 1) * owned :, :] = jnp.broadcast_to(rest[None], (shards,) + rest.shape)


def local_kernel(
    place_ref, got_ref, cot_ref, low_ref, mag_ref, early_cross, late_cross, out_ref, norm_ref
):
    dp, core = place_ref[0], place_ref[1]
    shards = got_ref.shape[0]
    columns = cot_ref.shape[1]
    rank = low_ref.shape[1]
    a_ref = low_ref.at[:, :, low_ref.shape[2] - columns :]
    owned = cot_ref.shape[0]
    tiles = columns // 128
    half = owned // 2
    at_extra = (2 * tiles + 1) * owned

    rests = [got_ref[source, at_extra:, :].astype(F32) for source in range(shards)]
    totals = []
    for k in range(3):
        sides = []
        for side in range(2):
            row = 4 * tiles + 3 * side + k
            parts = []
            for i in range(tiles if k < 2 else 1):
                at = (tiles * k + i) * owned + side * half
                total = None
                for source in range(shards):
                    value = decode(
                        got_ref[source, at : at + half, :], rests[source][row : row + 1, 0:1]
                    )
                    total = value if total is None else total + value
                parts.append(total)
            sides.append(jnp.concatenate(parts, axis=1) if k < 2 else parts[0])
        totals.append(jnp.concatenate(sides, axis=0))
    extra = rests[0]
    for source in range(1, shards):
        extra = extra + rests[source]
    pieces = extra[2 * tiles : 4 * tiles] + extra[: 2 * tiles]

    low = totals[2]
    low_hi, low_lo = split(low)
    outs, pres, scales = [], [], []
    for k in range(2):
        sq = jnp.concatenate(
            [pieces[tiles * k + i : tiles * k + i + 1] for i in range(tiles)], axis=1
        )
        norm = jnp.sqrt(sq + 1e-06)
        norm_ref[k : k + 1, :] = norm
        mine = slice(k * rank, (k + 1) * rank)
        pre = totals[k] + (dot(low_hi[:, mine], a_ref[k]) + dot(low_lo[:, mine], a_ref[k]))
        scale = mag_ref[k : k + 1, :] / norm
        pres.append(pre)
        scales.append(scale)
        outs.append(pre * scale)
    gate, up = outs
    quarter = half // 2
    cot = jnp.concatenate(
        [
            cot_ref[pl.ds(pl.multiple_of(start + side * quarter, quarter), quarter), :]
            for side in (core, 1 - core)
            for start in (0, half)
        ],
        axis=0,
    ).astype(F32)
    sig = 1.0 / (1.0 + jnp.exp(-gate))
    douts = (cot * up * sig * (1.0 + gate * (1.0 - sig)), cot * gate * sig)
    members = out_ref.shape[0]
    rows = 2 * rank // members
    codes, peaks, back_codes, back_peaks, ms = [], [], [], [], []
    for k in range(2):
        mine = slice(k * rank, (k + 1) * rank)
        ms.append(jnp.sum(douts[k] * pres[k], axis=0, keepdims=True))
        hi, lo = split(douts[k] * scales[k])
        grad_a = (
            dot(low_hi[:, mine], hi, TN) + dot(low_hi[:, mine], lo, TN) + dot(low_lo[:, mine], hi, TN)
        )
        back = dot(hi, a_ref[k], NT) + dot(lo, a_ref[k], NT)
        width = columns // 2
        lanes = pl.ds(pl.multiple_of(dp * width, width), width)
        cross = jnp.where(core == 1, early_cross[mine, lanes], late_cross[mine, lanes])
        peaks.append((peak_of(grad_a), peak_of(cross)))
        codes.append((encode(grad_a, peaks[k][0]), encode(cross, peaks[k][1])))
        back_peaks.append(peak_of(back))
        back_codes.append(encode(back, back_peaks[k]))
    m_peaks = [peak_of(m) for m in ms]
    m_codes = [
        encode(m, peak)[:, 128 * i : 128 * (i + 1)]
        for m, peak in zip(ms, m_peaks)
        for i in range(tiles)
    ]
    first_half = lax.broadcasted_iota(jnp.int32, (1, 128), 1) < 64
    pair = lambda x, y: jnp.where(first_half, x, y)
    ends = [pair(*back_peaks), pair(*m_peaks), jnp.zeros((1, 128), F32)]
    spare = m_codes[rows:]
    at_back = rows * (tiles + tiles // 2 + 1)
    for j in range(members):
        k, at = divmod(j * rows, rank)
        blocks = [
            code[at : at + rows, 128 * i : 128 * (i + 1)]
            for code in codes[k]
            for i in range(code.shape[1] // 128)
        ]
        blocks.append(jnp.concatenate(spare + [pair(*peaks[k])] + ends, axis=0))
        for i in range(0, len(blocks), 2):
            two = jnp.concatenate(blocks[i : i + 2], axis=0).astype(BF16)
            out_ref[j, rows * i : rows * (i + 2), :] = two
    rest = jnp.concatenate([jnp.concatenate(back_codes, axis=1)] + m_codes[:rows], axis=0).astype(BF16)
    out_ref[:, at_back:, :] = jnp.broadcast_to(rest[None], (members,) + rest.shape)


def packed(value):
    peak = peak_of(value)
    tail = jnp.broadcast_to(peak, (value.shape[0], 128))
    return jnp.concatenate([encode(value, peak), tail], axis=1).astype(BF16)


def unpacked(code):
    width = code.shape[1] - 128
    return decode(code[:, :width], code[0:1, width : width + 1].astype(F32))


def rows_kernel(place_ref, got_ref, coeff_ref, rows_ref):
    members = got_ref.shape[0]
    rows = rows_ref.shape[0]
    columns = coeff_ref.shape[1]
    tiles = columns // 128
    height = rows * (tiles + tiles // 2 + 1)
    coeff = jnp.where(place_ref[2] < 2, coeff_ref[0:1, :], coeff_ref[1:2, :])
    tokens = [jnp.zeros((rows, 128), F32)] * tiles
    crosses = [jnp.zeros((rows, 128), F32)] * tiles
    for j in range(members):
        blocks = got_ref[j, :height, :].astype(F32)
        peaks = blocks[height - 4 : height - 3]
        token = decode(blocks[: rows * tiles], peaks[:, 0:1])
        cross = decode(blocks[rows * tiles : height - rows], peaks[:, 64:65])
        for i in range(tiles):
            tokens[i] = tokens[i] + token[rows * i : rows * (i + 1)]
        first = j % 2 * (tiles // 2)
        for i in range(tiles // 2):
            crosses[first + i] = crosses[first + i] + cross[rows * i : rows * (i + 1)]
    own = jnp.concatenate(tokens, axis=1) + jnp.concatenate(crosses, axis=1) * coeff
    rows_ref[...] = packed(own)


def width_kernel(
    place_ref, got_ref, norm_ref, mag_ref, own_ref, other_ref, base_ref, low_ref,
    mine_ref, theirs_ref, grad_m_ref, coeff_ref, sum_ref,
):
    dp, core = place_ref[0], place_ref[1]
    members = got_ref.shape[0]
    shards = members // 2
    depth, columns = base_ref.shape[1:]
    rank = low_ref.shape[1]
    tiles = columns // 128
    owned = 2 * own_ref.shape[0] // shards
    half = owned // 2
    height = got_ref.shape[1]
    at_back = height - 8 - owned
    line = lax.broadcasted_iota(jnp.int32, (2 * tiles, 1), 0)
    m = None
    for j in range(members):
        ends = got_ref[j, at_back - 16 : at_back, :].astype(F32)[8:]
        code = jnp.concatenate([got_ref[j, height - 8 :, :].astype(F32), ends[:4]], axis=0)
        part = decode(code, jnp.where(line < tiles, ends[6:7, 0:1], ends[6:7, 64:65]))
        m = part if m is None else m + part
    for k in range(2):
        norm = norm_ref[k : k + 1, :]
        m_row = jnp.concatenate([m[tiles * k + i : tiles * k + i + 1] for i in range(tiles)], axis=1)
        grad_m = m_row / norm
        grad_m_ref[k : k + 1, :] = grad_m
        coeff_ref[k : k + 1, :] = -grad_m * mag_ref[k : k + 1, :] / (norm * norm)
    backs = []
    lane = lax.broadcasted_iota(jnp.int32, (1, 2 * rank), 1)
    for j in range(shards):
        source = member_of(j) * 2 + dp
        ends = got_ref[source, at_back - 16 : at_back, :].astype(F32)
        peak = jnp.where(lane < rank, ends[13:14, 0:1], ends[13:14, 64:65])
        backs.append(decode(got_ref[source, at_back : at_back + owned, :], peak))
    total = None
    for side, ref in enumerate((own_ref, other_ref)):
        back = jnp.concatenate([b[side * half : (side + 1) * half] for b in backs], axis=0)
        hi, lo = split(back)
        both = dot(jnp.concatenate([hi, lo], axis=1), ref[...], TN)
        part = both[: 2 * rank] + both[2 * rank :]
        total = part if total is None else total + part
    sum_ref[...] = total
    a = low_ref[dp, :, depth:]
    bt = low_ref[dp, :, :depth]
    hi, lo = split(a.astype(F32) * coeff_ref[pl.ds(dp, 1), :])
    weighted = jnp.concatenate([hi, lo], axis=0)
    both = dot(weighted, base_ref[dp], NT)
    small = dot(weighted, a, NT)
    small_hi, small_lo = split(small[:rank] + small[rank:])
    value = (both[:rank] + both[rank:]) + (dot(small_hi, bt) + dot(small_lo, bt))
    mine = pl.ds(pl.multiple_of(dp * rank, rank), rank)
    sum_ref[mine, :] += value
    width = mine_ref.shape[1]
    mine_ref[...] = sum_ref[:, pl.ds(pl.multiple_of(core * width, width), width)]
    theirs_ref[...] = sum_ref[:, pl.ds(pl.multiple_of((1 - core) * width, width), width)]


def sum_kernel(mine_ref, theirs_ref, out_ref):
    zs, rows, lanes = out_ref.shape
    part = mine_ref[...] + theirs_ref[...]
    peak = peak_of(part)
    out_ref[:, :, : lanes - 128] = encode(part, peak).reshape(zs, rows, lanes - 128).astype(BF16)
    out_ref[:, :, lanes - 128 :] = jnp.broadcast_to(peak, (zs, rows, 128)).astype(BF16)


def decoded(got_ref):
    lanes = got_ref.shape[2] - 128
    peaks = got_ref[:, :, lanes:].astype(F32)
    return decode(got_ref[:, :, :lanes], peaks[:, 0:1, 0:1])


def piece_kernel(got_ref, rows_ref, far_ref, out_ref):
    width = got_ref.shape[2]
    lanes = rows_ref.shape[1]
    out_ref[:, :width] = packed(jnp.sum(decoded(got_ref), axis=0))
    out_ref[:, width : width + lanes] = rows_ref[...]
    out_ref[:, width + lanes :] = far_ref[...]


def spread_kernel(mine_ref, theirs_ref, out_ref, rows_ref):
    width = out_ref.shape[2]
    lanes = rows_ref.shape[1] // 2
    code = packed(unpacked(mine_ref[:, :width]) + unpacked(theirs_ref[:, :width]))
    out_ref[...] = jnp.broadcast_to(code[None], out_ref.shape)
    rows_ref[:, :lanes] = mine_ref[:, width:]
    rows_ref[:, lanes:] = theirs_ref[:, width:]


def last_kernel(place_ref, own_ref, other_ref, r0_ref, r1_ref, r2_ref, r3_ref, grad_a_ref, grad_b_ref):
    core, member = place_ref[1], place_ref[3]
    count = own_ref.shape[1]
    lanes = r0_ref.shape[1] // 4
    for near, ref in enumerate((r0_ref, r1_ref, r2_ref, r3_ref)):
        for i, far in enumerate((0, 8, 1, 9)):
            at = pl.multiple_of(jnp.bitwise_xor(member, 2 * near + far) * count, count)
            grad_a_ref[pl.ds(at, count), :] = unpacked(ref[:, lanes * i : lanes * (i + 1)])
    rows, columns = grad_b_ref.shape
    width = columns // 2
    for side, ref in ((core, own_ref), (1 - core, other_ref)):
        lanes = pl.ds(pl.multiple_of(side * width, width), width)
        grad_b_ref[:, lanes] = decoded(ref).reshape(rows, width)


def call(kernel, outs, in_specs, flops=0, size=0, scratch=()):
    return pl.pallas_call(
        kernel,
        out_shape=outs,
        in_specs=in_specs,
        out_specs=[VMEM] * len(outs) if isinstance(outs, (list, tuple)) else VMEM,
        scratch_shapes=scratch,
        compiler_params=pltpu.CompilerParams(vmem_limit_bytes=24 * 2**20),
        cost_estimate=pl.CostEstimate(flops=flops, bytes_accessed=size, transcendentals=0),
    )


def shape(dims, dtype=F32):
    return jax.ShapeDtypeStruct(dims, dtype)


def per_device(tokens, base, b, a, magnitude, cotangent):
    dp = lax.axis_index("dp")
    core = lax.axis_index("core")
    depth, columns = base.shape[1:]
    rank = a.shape[1]
    shards = lax.axis_size(WIDTH)
    members = 2 * shards
    zs = lax.axis_size("z")
    own = 2 * zs * tokens.shape[0] // shards
    rows = 2 * rank // members
    tiles = columns // 128
    swap = [(0, 1), (1, 0)]
    low = jnp.concatenate([jnp.swapaxes(b, 1, 2), a], axis=2)
    place = jnp.stack([dp, core, lax.axis_index("x"), lax.axis_index(GROUP)]).astype(jnp.int32)

    g_own = lax.all_gather(tokens, "z", axis=0, tiled=True)
    g_own, place = lax.optimization_barrier((g_own, place))
    info_rows = 4 * tiles + 8
    outs = [
        shape((shards, (2 * tiles + 1) * own // 2, 128), BF16),
        shape((2 * rank, columns)),
        shape((info_rows, 128)),
    ]
    early, late = (
        functools.partial(
            call,
            kernel,
            outs,
            [SMEM] + [VMEM] * 3,
            flops=2**30,
            size=4 * 2**20,
        )()
        for kernel in (early_kernel, late_kernel)
    )
    first = early(place, g_own, base, low)
    g_own, first = lax.optimization_barrier((g_own, first))
    g_other = lax.ppermute(g_own, "core", swap)
    second = late(place, g_own, base, low)
    payload = call(
        forward_kernel,
        shape((shards, (2 * tiles + 1) * own + info_rows, 128), BF16),
        [SMEM] + [VMEM] * 7,
        flops=2**30,
        size=8 * 2**20,
        scratch=[pltpu.VMEM((info_rows, 128), F32)],
    )(place, first[0], first[2], second[0], second[2], g_other, base, low)
    got = lax.all_to_all(payload, WIDTH, 0, 0)

    height = rows * (tiles + tiles // 2 + 1) + own + 8
    sends, norm = call(
        local_kernel,
        [shape((members, height, 128), BF16), shape((2, columns))],
        [SMEM] + [VMEM] * 6,
        flops=2**27,
        size=4 * 2**20,
    )(place, got, cotangent, low, magnitude, first[1], second[1])
    got = lax.all_to_all(sends, GROUP, 0, 0)

    mine, theirs, grad_m, coeff = call(
        width_kernel,
        [shape((2 * rank, depth // 2))] * 2 + [shape((2, columns))] * 2,
        [SMEM] + [VMEM] * 7,
        flops=2**30,
        size=8 * 2**20,
        scratch=[pltpu.VMEM((2 * rank, depth), F32)],
    )(place, got, norm, magnitude, g_own, g_other, base, low)
    a_rows = call(
        rows_kernel,
        shape((rows, columns + 128), BF16),
        [SMEM] + [VMEM] * 2,
        flops=2**22,
        size=2**20,
    )(place, got, coeff)

    theirs = lax.ppermute(theirs, "core", swap)
    dims = (zs, 2 * rank // zs, depth // 2 + 128)
    chunks = call(sum_kernel, shape(dims, BF16), [VMEM] * 2, size=2**20)(mine, theirs)
    got = lax.all_to_all(chunks, "z", 0, 0)

    def across(value, flip):
        return lax.ppermute(value, ("y", "x"), [(i, i ^ flip) for i in range(shards)])

    piece = call(
        piece_kernel, shape((rows, dims[2] + 2 * (columns + 128)), BF16), [VMEM] * 3, size=2**18
    )(got, a_rows, across(a_rows, 2))
    theirs = lax.ppermute(piece, "dp", swap)
    chunks, near = call(
        spread_kernel, [shape(dims, BF16), shape((rows, 4 * (columns + 128)), BF16)], [VMEM] * 2, size=2**18
    )(piece, theirs)
    full = lax.all_to_all(chunks, "z", 0, 0)
    full, *near = lax.optimization_barrier((full, near, across(near, 4), across(near, 1), across(near, 5)))
    other = lax.ppermute(full, "core", swap)
    grad_a, grad_b = call(
        last_kernel,
        [shape((2 * rank, columns)), shape((2 * rank, depth))],
        [SMEM] + [VMEM] * 6,
        size=2**21,
    )(place, full, other, *near)
    grad_b = jnp.swapaxes(grad_b.reshape(2, rank, depth), 1, 2)
    return grad_a.reshape(2, rank, columns), grad_b, grad_m


def solution(mesh):
    sizes = mesh.shape
    fine = Mesh(
        mesh.devices.reshape(sizes["dp"], sizes["fsdp"] // 2, 2, 2, sizes["tensor"] // 2),
        ("dp", "z", "core", "y", "x"),
    )
    fsdp, tensor = ("z", "core"), ("y", "x")
    return jax.shard_map(
        per_device,
        mesh=fine,
        in_specs=(
            P(("dp",) + fsdp, tensor),
            P(None, tensor, fsdp),
            P(None, tensor, None),
            P(None, None, fsdp),
            P(None, fsdp),
            P(("dp",) + tensor, fsdp),
        ),
        out_specs=(P(None, None, fsdp), P(None, tensor, None), P(None, fsdp)),
        check_vma=False,
    )
```
